32 devices in a mesh: gx: 2 (over y), gy: 4 (over x, core), gz: 4 (over z).
Axes of the slice: x: 2, y: 2, z: 4, core: 2. Of those that a mesh axis runs over, the one named last changes fastest.
Arguments:
- inputs: bfloat16 [640, 12288], P(('gy', 'gz'), 'gx'), may hold values from -6 to 6
- pre_act: bfloat16 [640, 24576], P('gx', ('gy', 'gz')), may hold values from -6 to 6
- out_grad: bfloat16 [640, 12288], P(('gy', 'gz'), 'gx'), may hold values from -6 to 6
- w_in: bfloat16 [12288, 24576], P('gx', ('gy', 'gz')), may hold values from -0.0546875 to 0.0546875
- w_out: bfloat16 [24576, 12288], P(('gy', 'gz'), 'gx'), may hold values from -0.0390625 to 0.0390625
Outputs:
- in_grad: bfloat16 [640, 12288], P(('gy', 'gz'), 'gx')
- w_in_grad: bfloat16 [12288, 24576], P('gx', ('gy', 'gz'))
- w_out_grad: bfloat16 [24576, 12288], P(('gy', 'gz'), 'gx')
The draws below stay inside these ranges and needn't reach their ends.
All inputs are finite; a program needn't handle non-finite values.
Results may differ from the reference program's by a relative error of at most 0.0051.
Values may be sent and summed in bfloat16 or wider, within the bound.
No kernel may reach another device: no remote copies, remote signals or barrier semaphores. Data moves between devices by JAX's collectives and lax.ppermute only.
A program may use at most 192 MiB of HBM per device.

```python
import math
import jax
import jax.numpy as jnp
from jax import lax

D = 12288
FF = 24576
TOKENS = 640


def block_scale(stream_key, shape, cuts, smallest, top_value):
    level = 1.0
    for position, shards_of in cuts:
        steps = jax.random.uniform(jax.random.fold_in(jax.random.fold_in(stream_key, 6), position), (shards_of,), jnp.float32, smallest / len(cuts), top_value / len(cuts))
        level = level * jnp.repeat(jnp.exp(steps), shape[position] // shards_of).reshape((-1,) + (1,) * (len(shape) - 1 - position))
    return level


def scatter_about(key, shape, scale, limit, shards=(), held_as=jnp.bfloat16):
    values = jax.random.normal(key, shape, jnp.float32) * scale
    if len(shards) > 0:
        values = block_scale(key, shape, shards, -0.22, 0.18) * values
    return jnp.clip(values, min=-limit, max=limit).astype(held_as)


def setup_inputs(seed: int = 0) -> dict:
    arg_keys = jax.random.split(jax.random.key(seed), 6)
    return {
        "inputs": scatter_about(arg_keys[0], (TOKENS, D), 1.0, 6.0, ((0, 16), (1, 2))),
        "pre_act": scatter_about(arg_keys[1], (TOKENS, FF), 1.0, 6.0, ((0, 2), (1, 16))),
        "out_grad": scatter_about(arg_keys[2], (TOKENS, D), 1.0, 6.0, ((0, 16), (1, 2))),
        "w_in": scatter_about(arg_keys[3], (D, FF), D ** -0.5, 0.0546875, ((0, 2), (1, 16))),
        "w_out": scatter_about(arg_keys[4], (FF, D), FF ** -0.5, 0.0390625, ((0, 16), (1, 2))),
    }


def gelu_parts(pre_values):
    values = pre_values.astype(jnp.float32)
    normal_cdf = 0.5 * (1.0 + lax.erf(values / math.sqrt(2.0)))
    activity = values * normal_cdf
    slope = normal_cdf + values * jnp.exp(-0.5 * values * values) / math.sqrt(2.0 * math.pi)
    return (activity, slope)

def reference(inputs, pre_act, out_grad, w_in, w_out):
    grad_act = jnp.dot(out_grad, w_out.T, preferred_element_type=jnp.float32)
    activity, slope = gelu_parts(pre_act)
    act_low = activity.astype(jnp.bfloat16)
    grad_pre = (grad_act * slope).astype(jnp.bfloat16)
    in_grad = jnp.dot(grad_pre, w_in.T, preferred_element_type=jnp.float32).astype(jnp.bfloat16)
    factor = 1.0 / math.sqrt(TOKENS)
    w_in_grad = (jnp.dot(inputs.T, grad_pre, preferred_element_type=jnp.float32) * factor).astype(jnp.bfloat16)
    w_out_grad = (jnp.dot(act_low.T, out_grad, preferred_element_type=jnp.float32) * factor).astype(jnp.bfloat16)
    return (in_grad, w_in_grad, w_out_grad)
```

```python
import math

import jax
import jax.numpy as jnp
from jax import lax
from jax.sharding import PartitionSpec as P

RING = ("gy", "gz")


def gelu_parts(pre_values):
    values = pre_values.astype(jnp.float32)
    normal_cdf = 0.5 * (1.0 + lax.erf(values / math.sqrt(2.0)))
    activity = values * normal_cdf
    slope = normal_cdf + values * jnp.exp(-0.5 * values * values) / math.sqrt(2.0 * math.pi)
    return (activity, slope)


def right_trans(left, right):
    return lax.dot_general(
        left, right, (((1,), (1,)), ((), ())), preferred_element_type=jnp.float32
    )


def left_trans(left, right):
    return lax.dot_general(
        left, right, (((0,), (0,)), ((), ())), preferred_element_type=jnp.float32
    )


class Ring:
    def __init__(self, gy, gz):
        self.cores = 2 if gy % 2 == 0 else 1
        chips = []
        for x in range(gy // self.cores):
            line = range(gz) if x % 2 == 0 else reversed(range(gz))
            chips += [(x, z) for z in line]
        self.size = len(chips)
        self.half = self.size // 2
        self.even = self.size % 2 == 0
        self.rank = [
            [(x * self.cores + core) * gz + z for core in range(self.cores)] for x, z in chips
        ]

    def shift(self, by):
        pairs = []
        for place in range(self.size):
            target = (place + by) % self.size
            for core in range(self.cores):
                pairs.append((self.rank[place][core], self.rank[target][core]))
        return pairs

    def swap(self):
        return [(ranks[core], ranks[1 - core]) for ranks in self.rank for core in range(2)]

    def groups(self):
        if self.half < 4:
            return [list(range(self.half + 1))]
        middle = [[step] for step in range(2, self.half - 1)]
        return [[0, 1]] + middle + [[self.half - 1, self.half]]

    def offsets(self, step):
        if step == 0:
            return [0]
        if step == self.half and self.even:
            return [self.half]
        return [-step, step]


def gather_steps(ring, block):
    held = {0: block}
    left, right = block, block
    for step in range(1, ring.half + 1):
        if step == ring.half and ring.even:
            cut = block.shape[1] // 2
            low = lax.ppermute(left[:, :cut], RING, ring.shift(1))
            high = lax.ppermute(right[:, cut:], RING, ring.shift(-1))
            held[step] = jnp.concatenate([low, high], axis=1)
        else:
            left = lax.ppermute(left, RING, ring.shift(1))
            right = lax.ppermute(right, RING, ring.shift(-1))
            held[-step], held[step] = left, right
    return held


def with_other_core(ring, mine):
    if ring.cores == 1:
        return mine
    theirs = lax.ppermute(mine, RING, ring.swap())
    return jnp.concatenate([mine, theirs], axis=0)


def exchange(values, axis):
    size = lax.axis_size(axis)
    return [
        lax.ppermute(values, axis, [(i, (i + by) % size) for i in range(size)])
        for by in range(1, size)
    ]


def shards(inputs, pre_act, out_grad, w_in, w_out):
    ring = Ring(lax.axis_size("gy"), lax.axis_size("gz"))
    rows = inputs.shape[0]
    groups = ring.size * ring.cores
    factor = 1.0 / math.sqrt(rows * groups)
    rank = lax.axis_index(RING)
    core = lax.rem(lax.axis_index("gy"), ring.cores)
    place_of = [0] * groups
    for place, ranks in enumerate(ring.rank):
        for one in ranks:
            place_of[one] = place
    place = jnp.array(place_of, jnp.int32)[rank]
    ranks = jnp.array(ring.rank, jnp.int32)

    size_x = lax.axis_size("gx")
    me_x = lax.axis_index("gx")
    full_pre = jnp.zeros((size_x * pre_act.shape[0], pre_act.shape[1]), pre_act.dtype)
    full_pre = lax.dynamic_update_slice(full_pre, pre_act, (me_x * pre_act.shape[0], 0))
    for by, got in enumerate(exchange(pre_act, "gx"), 1):
        owner = lax.rem(me_x - by + size_x, size_x)
        full_pre = lax.dynamic_update_slice(full_pre, got, (owner * pre_act.shape[0], 0))

    order = [[o for step in group for o in ring.offsets(step)] for group in ring.groups()]

    def ordered(full, offsets):
        blocks = []
        for which in range(ring.cores):
            for offset in offsets:
                at = lax.rem(place + offset + ring.size, ring.size)
                owner = ranks[at, lax.rem(core + which, ring.cores)]
                blocks.append(lax.dynamic_slice_in_dim(full, owner * rows, rows, 0))
        return jnp.concatenate(blocks, axis=0)

    grads = gather_steps(ring, out_grad)
    tokens, acts, pres = [], [], []
    for offsets in order:
        chunk = with_other_core(ring, jnp.concatenate([grads[o] for o in offsets], axis=0))
        partial = right_trans(chunk, w_out)
        total = partial
        for got in exchange(partial.astype(jnp.bfloat16), "gx"):
            total = total + got.astype(jnp.float32)
        activity, slope = gelu_parts(ordered(full_pre, offsets))
        tokens.append(chunk)
        acts.append(activity.astype(jnp.bfloat16))
        pres.append((total * slope).astype(jnp.bfloat16))

    sums = {}
    for offsets, pre in reversed(list(zip(order, pres))):
        part = right_trans(pre, w_in)
        count = len(offsets) * rows
        mine = part[:count]
        if ring.cores == 2:
            mine = mine + lax.ppermute(
                part[count:].astype(jnp.bfloat16), RING, ring.swap()
            ).astype(jnp.float32)
        for i, offset in enumerate(offsets):
            sums[offset] = mine[i * rows : (i + 1) * rows]

    low = jnp.bfloat16
    right = left = None
    for step in range(ring.half, 0, -1):
        if step == ring.half and ring.even:
            cut = out_grad.shape[1] // 2
            here = sums[step].astype(low)
            right = lax.ppermute(here[:, :cut], RING, ring.shift(1)).astype(jnp.float32)
            left = lax.ppermute(here[:, cut:], RING, ring.shift(-1)).astype(jnp.float32)
            right = jnp.pad(right, ((0, 0), (0, right.shape[1])))
            left = jnp.pad(left, ((0, 0), (left.shape[1], 0)))
        else:
            go_right, go_left = sums[step], sums[-step]
            if right is not None:
                go_right, go_left = go_right + right, go_left + left
            right = lax.ppermute(go_right.astype(low), RING, ring.shift(1)).astype(jnp.float32)
            left = lax.ppermute(go_left.astype(low), RING, ring.shift(-1)).astype(jnp.float32)
    in_grad = (sums[0] + right + left).astype(jnp.bfloat16)

    w_out_grad = left_trans(jnp.concatenate(acts, axis=0), jnp.concatenate(tokens, axis=0))
    w_out_grad = (w_out_grad * factor).astype(jnp.bfloat16)

    held = gather_steps(ring, inputs)
    mine = jnp.concatenate([held[o] for offsets in order for o in offsets], axis=0)
    theirs = lax.ppermute(mine, RING, ring.swap()) if ring.cores == 2 else None
    pieces, at = [], 0
    for offsets in order:
        count = len(offsets) * rows
        pieces.append(mine[at : at + count])
        if theirs is not None:
            pieces.append(theirs[at : at + count])
        at += count
    w_in_grad = left_trans(jnp.concatenate(pieces, axis=0), jnp.concatenate(pres, axis=0))
    w_in_grad = (w_in_grad * factor).astype(jnp.bfloat16)
    return (in_grad, w_in_grad, w_out_grad)


def solution(mesh):
    placed = (
        P(("gy", "gz"), "gx"),
        P("gx", ("gy", "gz")),
        P(("gy", "gz"), "gx"),
        P("gx", ("gy", "gz")),
        P(("gy", "gz"), "gx"),
    )
    return jax.shard_map(
        shards,
        mesh=mesh,
        in_specs=placed,
        out_specs=(P(("gy", "gz"), "gx"), P("gx", ("gy", "gz")), P(("gy", "gz"), "gx")),
        check_vma=False,
    )
```

```python
import math

import jax
import jax.numpy as jnp
from jax import lax
from jax.experimental import pallas as pl
from jax.experimental.pallas import tpu as pltpu
from jax.sharding import PartitionSpec as P

RING = ("gy", "gz")


class Ring:
    def __init__(self, gy, gz):
        self.cores = 2 if gy % 2 == 0 else 1
        chips = []
        for x in range(gy // self.cores):
            line = range(gz) if x % 2 == 0 else reversed(range(gz))
            chips += [(x, z) for z in line]
        self.size, self.line = len(chips), gz
        self.half = self.size // 2
        self.even = self.size % 2 == 0
        self.rank = [
            [(x * self.cores + core) * gz + z for core in range(self.cores)] for x, z in chips
        ]

    def place(self, x, z):
        return x * self.line + jnp.where(x % 2 == 0, z, self.line - 1 - z)

    def rank_at(self, place, core):
        x, z = place // self.line, place % self.line
        return (x * 2 + core) * self.line + jnp.where(x % 2 == 0, z, self.line - 1 - z)

    def shift(self, by):
        pairs = []
        for place in range(self.size):
            target = (place + by) % self.size
            for core in range(self.cores):
                pairs.append((self.rank[place][core], self.rank[target][core]))
        return pairs

    def swap(self):
        return [(ranks[core], ranks[1 - core]) for ranks in self.rank for core in range(2)]

    def groups(self):
        cut = max(self.half - 1, 1)
        return [list(range(cut)), list(range(cut, self.half + 1))]

    def offsets(self, step):
        if step == 0:
            return [0]
        if step == self.half and self.even:
            return [self.half]
        return [-step, step]


def gelu_parts(values):
    normal_cdf = 0.5 * (1.0 + lax.erf(values / math.sqrt(2.0)))
    activity = values * normal_cdf
    slope = normal_cdf + values * jnp.exp(-0.5 * values * values) / math.sqrt(2.0 * math.pi)
    return (activity, slope)


def right_trans(left, right):
    return lax.dot_general(
        left, right, (((1,), (1,)), ((), ())), preferred_element_type=jnp.float32
    )


def left_trans(left, right):
    return lax.dot_general(
        left, right, (((0,), (0,)), ((), ())), preferred_element_type=jnp.float32
    )


VMEM = pl.BlockSpec(memory_space=pltpu.VMEM)
SMEM = pl.BlockSpec(memory_space=pltpu.SMEM)
MIB = 1 << 20


def shape(rows, columns, dtype=jnp.bfloat16):
    return jax.ShapeDtypeStruct((rows, columns), dtype)


def in_hbm(rows, columns, dtype=jnp.bfloat16):
    return pltpu.HBM((rows, columns), dtype)


def constrained(arrays):
    return [pltpu.with_memory_space_constraint(each, pltpu.HBM) for each in arrays]


def cost(flops, moved, exps=0):
    return pl.CostEstimate(flops=flops, bytes_accessed=moved, transcendentals=exps)


def tile_of(total, most):
    for tile in range(most, 127, -128):
        if total % tile == 0:
            return tile
    return total


def gelu_call(ring, pres, offsets, rows):
    held, hidden = pres[0].shape
    many, count = sum(each.shape[0] for each in pres) // held, 2 * len(offsets)

    def kernel(*refs):
        given, (act_ref, slope_ref, wide) = refs[:-3], refs[-3:]
        at = 0
        for ref in given:
            wide[at : at + ref.shape[0], :] = ref[...].astype(jnp.float32)
            at += ref.shape[0]
        me, gy = lax.axis_index("gx"), lax.axis_index("gy")
        place = ring.place(gy // 2, lax.axis_index("gz"))
        for block in range(count):
            which, offset = divmod(block, len(offsets))
            there = (place + offsets[offset] + ring.size) % ring.size
            rank = ring.rank_at(there, (gy + which) % 2)
            slot = (me - rank * rows // held + many) % many
            at = pl.multiple_of(slot * held + rank * rows % held, 8)
            activity, slope = gelu_parts(wide[pl.ds(at, rows), :])
            act_ref[block * rows : (block + 1) * rows, :] = activity.astype(act_ref.dtype)
            slope_ref[block * rows : (block + 1) * rows, :] = slope

    return pl.pallas_call(
        kernel,
        grid=(1,),
        in_specs=[VMEM] * len(pres),
        out_specs=[whole(count * rows, hidden)] * 2,
        out_shape=[in_hbm(count * rows, hidden), in_hbm(count * rows, hidden, jnp.float32)],
        scratch_shapes=[pltpu.VMEM((many * held, hidden), jnp.float32)],
        cost_estimate=cost(6000 * count * rows * hidden, 1),
        compiler_params=pltpu.CompilerParams(vmem_limit_bytes=10 * MIB),
        name="gelu",
    )(*pres)


def hold_call(weights):
    rows = weights.shape[0]
    cut = rows // 4
    weights = pltpu.with_memory_space_constraint(weights, pltpu.HBM)

    def kernel(weight_ref, out_ref, here_ref, sems):
        here_ref[...] = jnp.zeros_like(here_ref)
        copies = [
            pltpu.make_async_copy(
                weight_ref.at[pl.ds(i * cut, cut)], out_ref.at[pl.ds(i * cut, cut)], sems.at[i]
            )
            for i in range(4)
        ]
        for copy in copies:
            copy.start()
        for copy in copies:
            copy.wait()

    return pl.pallas_call(
        kernel,
        in_specs=[pl.BlockSpec(memory_space=pl.ANY)],
        out_specs=[VMEM] * 2,
        out_shape=[pltpu.VMEM(weights.shape, weights.dtype), shape(8, 128, jnp.float32)],
        scratch_shapes=[pltpu.SemaphoreType.DMA((4,))],
        cost_estimate=cost(1, 1),
        compiler_params=pltpu.CompilerParams(vmem_limit_bytes=10 * MIB),
        name="hold",
    )(weights)


def whole(rows, columns):
    return pl.BlockSpec((rows, columns), lambda i: (0, 0), pipeline_mode=pl.Buffered(1))


def split_call(left, right, cut):
    def kernel(left_ref, right_ref, low_ref, high_ref):
        low_ref[...] = left_ref[:, :cut]
        high_ref[...] = right_ref[:, cut:]

    rows, width = left.shape
    return pl.pallas_call(
        kernel,
        in_specs=[VMEM] * 2,
        out_specs=[VMEM] * 2,
        out_shape=[shape(rows, cut), shape(rows, width - cut)],
        cost_estimate=cost(1, 1),
        compiler_params=pltpu.CompilerParams(vmem_limit_bytes=10 * MIB),
        name="split",
    )(left, right)


def parts_call(values):
    rows, width = values.shape
    cut = rows * 2 // 5 // 16 * 16

    def kernel(ref, upper_ref, lower_ref):
        upper_ref[...] = ref[:cut, :]
        lower_ref[...] = ref[cut:, :]

    return pl.pallas_call(
        kernel,
        in_specs=[VMEM],
        out_specs=[VMEM] * 2,
        out_shape=[shape(cut, width), shape(rows - cut, width)],
        cost_estimate=cost(1, 1),
        compiler_params=pltpu.CompilerParams(vmem_limit_bytes=10 * MIB),
        name="parts",
    )(values)


def pack_call(blocks, rows, width):
    flat = [piece for block in blocks for piece in block]

    def kernel(*refs):
        given, out_ref = iter(refs), refs[-1]
        for i, block in enumerate(blocks):
            at = 0
            for piece in block:
                size = piece.shape[1]
                out_ref[i * rows : (i + 1) * rows, at : at + size] = next(given)[...]
                at += size

    return pl.pallas_call(
        kernel,
        grid=(1,),
        in_specs=[VMEM] * len(flat),
        out_specs=whole(len(blocks) * rows, width),
        out_shape=in_hbm(len(blocks) * rows, width),
        cost_estimate=cost(1, 1),
        compiler_params=pltpu.CompilerParams(vmem_limit_bytes=8 * MIB),
        name="pack",
    )(*flat)


def add_call(mine, theirs, places, arrived, rows, outs):
    width = mine.shape[1]
    flat = [value for block in arrived for value, _ in block]

    def kernel(*refs):
        wide, theirs_ref = refs[: len(places)], refs[len(places)]
        given = iter(refs[len(places) + 1 : len(refs) - len(outs) - len(places)])
        made = refs[len(refs) - len(places) :]
        for i, (place, block) in enumerate(zip(places, arrived)):
            at = slice(place * rows, (place + 1) * rows)
            made[i][...] = wide[i][...] + theirs_ref[at, :].astype(jnp.float32)
            for value, first in block:
                columns = slice(first, first + value.shape[1])
                made[i][:, columns] += next(given)[...].astype(jnp.float32)
        for ref, (i, first, last) in zip(refs[-len(outs) - len(places) :], outs):
            ref[...] = made[i][:, first:last].astype(ref.dtype)

    return pl.pallas_call(
        kernel,
        grid=(1,),
        in_specs=[
            pl.BlockSpec((rows, width), lambda i, p=p: (p, 0), pipeline_mode=pl.Buffered(1))
            for p in places
        ]
        + [VMEM] * (1 + len(flat)),
        out_specs=[VMEM] * len(outs),
        out_shape=[shape(rows, last - first) for _, first, last in outs],
        scratch_shapes=[pltpu.VMEM((rows, width), jnp.float32)] * len(places),
        cost_estimate=cost(1, 1),
        compiler_params=pltpu.CompilerParams(vmem_limit_bytes=8 * MIB),
        name="add",
    )(*constrained([mine] * len(places)), theirs, *flat)


def grad_act_call(blocks, weights, rows, cuts):
    hidden, width = weights.shape
    flat = [piece for block in blocks for piece in block]
    count = len(blocks) * rows
    tile = tile_of(hidden, 256)
    steps = hidden // tile
    spans = list(zip([0] + cuts, cuts + [count]))

    def kernel(*refs):
        weight_ref, chunk_ref, part_ref, *low_refs, joined, sem = refs[len(flat) :]
        i = pl.program_id(0)
        copy = pltpu.make_async_copy(joined, chunk_ref, sem)

        @pl.when(i == 0)
        def _():
            given = iter(refs)
            for j, block in enumerate(blocks):
                at = 0
                for piece in block:
                    size = piece.shape[1]
                    joined[j * rows : (j + 1) * rows, at : at + size] = next(given)[...]
                    at += size
            copy.start()

        at = pl.ds(pl.multiple_of(i * tile, tile), tile)
        got = right_trans(joined[...], weight_ref[at, :])
        part_ref[...] = got
        for ref, (begin, end) in zip(low_refs, spans):
            ref[...] = got[begin:end].astype(ref.dtype)

        @pl.when(i == steps - 1)
        def _():
            copy.wait()

    return pl.pallas_call(
        kernel,
        grid=(steps,),
        in_specs=[VMEM] * (len(flat) + 1),
        out_specs=[
            pl.BlockSpec(memory_space=pl.ANY),
            pl.BlockSpec((count, tile), lambda i: (0, i)),
        ]
        + [pl.BlockSpec((end - begin, tile), lambda i: (0, i)) for begin, end in spans],
        out_shape=[in_hbm(count, width), in_hbm(count, hidden, jnp.float32)]
        + [shape(end - begin, hidden) for begin, end in spans],
        scratch_shapes=[pltpu.VMEM((count, width), jnp.bfloat16), pltpu.SemaphoreType.DMA],
        cost_estimate=cost(1, 1),
        compiler_params=pltpu.CompilerParams(vmem_limit_bytes=10 * MIB),
        name="grad_act",
    )(*flat, weights)


def in_grad_call(part, others, slope, weights):
    flat = [piece for pieces in zip(*others) for piece in pieces]
    width, hidden = weights.shape
    count = part.shape[0]
    half = count // 2
    tile = tile_of(width, 1024)

    def kernel(*refs):
        part_ref, slope_ref = refs[:2]
        weight_ref, pre_ref, mine_ref, theirs_ref = refs[-4:]
        i = pl.program_id(0)

        @pl.when(i == 0)
        def _():
            given, at = iter(refs[2:-4]), 0
            for pieces in zip(*others):
                here = slice(at, at + pieces[0].shape[0])
                total = part_ref[here, :]
                for _ in pieces:
                    total = total + next(given)[...].astype(jnp.float32)
                pre_ref[here, :] = (total * slope_ref[here, :]).astype(pre_ref.dtype)
                at = here.stop

        at = pl.ds(pl.multiple_of(i * tile, tile), tile)
        got = right_trans(pre_ref[...], weight_ref[at, :])
        mine_ref[...] = got[:half]
        theirs_ref[...] = got[half:].astype(theirs_ref.dtype)

    return pl.pallas_call(
        kernel,
        grid=(width // tile,),
        in_specs=[whole(count, hidden)] * 2 + [whole(*each.shape) for each in flat] + [VMEM],
        out_specs=[
            whole(count, hidden),
            pl.BlockSpec((half, tile), lambda i: (0, i)),
            pl.BlockSpec((half, tile), lambda i: (0, i)),
        ],
        out_shape=[
            in_hbm(count, hidden),
            in_hbm(half, width, jnp.float32),
            shape(half, width),
        ],
        cost_estimate=cost(1, 1),
        compiler_params=pltpu.CompilerParams(vmem_limit_bytes=14 * MIB),
        name="in_grad",
    )(part, slope, *flat, weights)


def pieces_of(width, most):
    tile = tile_of(width, 1024)
    tiles = width // tile
    calls = min(most, tiles)
    ends = [tiles * i // calls for i in range(calls + 1)]
    return tile, [(first, last - first) for first, last in zip(ends, ends[1:])]


def w_out_grad_call(acts, chunks, factor, tile, first, count, earlier):
    sizes = [chunk.shape[0] for chunk in chunks]
    many, total = len(sizes), sum(sizes)
    hidden, width = acts[0].shape[1], chunks[0].shape[1]

    def kernel(*refs):
        given, tokens, (out_ref, turned) = refs[:many], refs[many : 2 * many], refs[-2:]

        @pl.when(pl.program_id(0) == 0)
        def _():
            turned[...] = jnp.concatenate([ref[...] for ref in given], axis=0).T

        joined = jnp.concatenate([ref[...] for ref in tokens], axis=0)
        got = jnp.dot(turned[...], joined, preferred_element_type=jnp.float32)
        out_ref[...] = (got * factor).astype(out_ref.dtype)

    return pl.pallas_call(
        kernel,
        grid=(count,),
        in_specs=[whole(size, hidden) for size in sizes]
        + [pl.BlockSpec((size, tile), lambda i: (0, first + i)) for size in sizes]
        + [pl.BlockSpec(memory_space=pl.ANY)] * len(earlier),
        out_specs=pl.BlockSpec((hidden, tile), lambda i: (0, first + i)),
        out_shape=shape(hidden, width),
        input_output_aliases={2 * many: 0} if earlier else {},
        scratch_shapes=[pltpu.VMEM((hidden, total), jnp.bfloat16)],
        cost_estimate=cost(3 * total * tile * count * hidden, 2 * hidden * tile * count),
        compiler_params=pltpu.CompilerParams(vmem_limit_bytes=26 * MIB),
        name="w_out_grad",
    )(*acts, *chunks, *earlier)


def w_in_grad_call(blocks, pres, factor, tile, first, count, earlier):
    width = blocks[0].shape[1]
    many, sizes = len(blocks), [pre.shape[0] for pre in pres]
    total, hidden = sum(sizes), pres[0].shape[1]

    def kernel(*refs):
        given, wanted = refs[:many], refs[many : many + len(sizes)]
        out_ref, tokens, grads = refs[-3:]

        @pl.when(pl.program_id(0) == 0)
        def _():
            at = 0
            for ref, size in zip(wanted, sizes):
                grads[at : at + size, :] = ref[...]
                at += size

        at = 0
        for ref in given:
            tokens[at : at + ref.shape[0], :] = ref[...]
            at += ref.shape[0]
        got = left_trans(tokens[...], grads[...])
        out_ref[...] = (got * factor).astype(out_ref.dtype)

    return pl.pallas_call(
        kernel,
        grid=(count,),
        in_specs=[pl.BlockSpec((each.shape[0], tile), lambda i: (0, first + i)) for each in blocks]
        + [whole(size, hidden) for size in sizes]
        + [pl.BlockSpec(memory_space=pl.ANY)] * len(earlier),
        out_specs=pl.BlockSpec((tile, hidden), lambda i: (first + i, 0)),
        out_shape=shape(width, hidden),
        input_output_aliases={many + len(sizes): 0} if earlier else {},
        scratch_shapes=[
            pltpu.VMEM((total, tile), jnp.bfloat16),
            pltpu.VMEM((total, hidden), jnp.bfloat16),
        ],
        cost_estimate=cost(3 * total * tile * count * hidden, 2 * hidden * tile * count),
        compiler_params=pltpu.CompilerParams(vmem_limit_bytes=26 * MIB),
        name="w_in_grad",
    )(*blocks, *pres, *earlier)


def after(values, *others):
    return lax.optimization_barrier((values, others))[0]


class Gather:
    def __init__(self, ring, block, halve):
        self.ring, self.halve = ring, halve
        self.held = {0: [block]}
        self.left = self.right = block
        self.done = 0

    def step(self, *others):
        ring = self.ring
        self.done += 1
        left, right = self.left, self.right
        if others:
            left, right = after((left, right), *others)
        if self.done == ring.half and ring.even:
            if self.halve:
                cut = left.shape[1] // 2
                low, high = split_call(left, right, cut)
                low = lax.ppermute(low, RING, ring.shift(1))
                high = lax.ppermute(high, RING, ring.shift(-1))
                self.held[self.done] = [low, high]
            else:
                self.held[self.done] = [lax.ppermute(left, RING, ring.shift(1))]
        else:
            self.left = lax.ppermute(left, RING, ring.shift(1))
            self.right = lax.ppermute(right, RING, ring.shift(-1))
            self.held[-self.done], self.held[self.done] = [self.left], [self.right]


def other_core(ring, pieces):
    return [lax.ppermute(piece, RING, ring.swap()) for piece in pieces]


def exchange(values, axis):
    size = lax.axis_size(axis)
    return [
        lax.ppermute(values, axis, [(i, (i + by) % size) for i in range(size)])
        for by in range(1, size)
    ]


def shards(inputs, pre_act, out_grad, w_in, w_out):
    ring = Ring(lax.axis_size("gy"), lax.axis_size("gz"))
    assert ring.cores == 2
    rows, width = inputs.shape
    groups = ring.size * 2
    factor = 1.0 / math.sqrt(rows * groups)
    order = [[o for step in group for o in ring.offsets(step)] for group in ring.groups()]

    w_out, here = hold_call(w_out)
    upper, lower = parts_call(pre_act)
    came = [exchange(upper, "gx")]

    grads = Gather(ring, out_grad, True)
    chunks, partials, swapped = [], [], {0: other_core(ring, grads.held[0])}
    for number, offsets in enumerate(order):
        first, last = ring.groups()[number][0], ring.groups()[number][-1]
        while grads.done < last:
            if number > 0 and grads.done >= first:
                grads.step(sent)
            elif grads.done == 1:
                grads.step(here, came[0], swapped[0])
                came.append(exchange(after(lower, came[0], here), "gx"))
            else:
                earlier = [each for offset, each in swapped.items() if abs(offset) < grads.done]
                grads.step(*([earlier, came] if grads.done > 1 else []))
            if number > 0 and grads.done == last:
                pres_x = [pre_act] + [each for pieces in zip(*came) for each in pieces]
                ready = after(pres_x, sent)
                acts, slopes = zip(*[gelu_call(ring, ready, each, rows) for each in order])
            for offset in ring.offsets(grads.done):
                ahead = here if number == 0 else slopes if grads.done == last else sent
                swapped[offset] = other_core(ring, after(grads.held[offset], ahead))
        blocks = [grads.held[o] for o in offsets] + [swapped[o] for o in offsets]
        cuts = [2 * len(blocks) * rows // 5 // 16 * 16] if number == 0 else []
        chunk, partial, *sent = grad_act_call(blocks, w_out, rows, cuts)
        chunks.append(chunk)
        partials.append(partial)
        if number == 0:
            early, late = exchange(sent[0], "gx"), sent[1]
    received = [[each] for each in exchange(sent[0], "gx")]

    tokens = Gather(ring, after(inputs, grads.held[ring.half], swapped), True)
    chunks = constrained(chunks)

    def advance(*others):
        arrived = list(tokens.held.values())[1:]
        if tokens.done < ring.half:
            tokens.step(*others)
        return arrived

    tile, out_cuts = pieces_of(width, 3)
    tile, in_cuts = pieces_of(width, 2)
    w_out_grad, w_in_grad = [], []

    def w_out_piece(*others):
        nonlocal w_out_grad
        first, count = out_cuts.pop(0)
        given = [after(acts[0], *others)] + list(acts[1:])
        w_out_grad = [w_out_grad_call(given, chunks, factor, tile, first, count, w_out_grad)]
        return w_out_grad

    def w_in_piece(*others):
        nonlocal w_in_grad
        first, count = in_cuts.pop(0)
        flat = [each for number in range(len(order)) for each in packed[number]]
        given = constrained([after(pres[0], *others)] + pres[1:])
        w_in_grad = [w_in_grad_call(flat, given, factor, tile, first, count, w_in_grad)]
        return w_in_grad

    w_out_piece(advance(), early)
    arrived = advance()
    w_in = pltpu.with_memory_space_constraint(w_in, pltpu.VMEM)
    if len(out_cuts) > 1:
        w_out_piece(arrived)

    sums, pres = {}, [None] * len(order)

    def in_grad_chunk(i, received, *others):
        partial = after(partials[i], *others)
        pres[i], mine, theirs = in_grad_call(partial, received, slopes[i], w_in)
        return mine, theirs

    def swap_sums(i, mine, theirs):
        got = lax.ppermute(theirs, RING, ring.swap())
        for j, offset in enumerate(order[i]):
            sums[offset] = (mine, got, j)

    def add(offsets, arrived, outs, *others):
        mine, theirs, _ = sums[offsets[0]]
        places = [sums[offset][2] for offset in offsets]
        return add_call(mine, after(theirs, *others), places, arrived, rows, outs)

    packed = {}

    def pack(number, *others):
        blocks = after([tokens.held[o] for o in order[number]], *others)
        packed[number] = [pack_call(blocks, rows, width)]
        return packed[number]

    mine, theirs = in_grad_chunk(1, received, w_out_grad, advance())
    swap_sums(1, mine, theirs)
    right, left, beside = [], [], []
    for step in range(ring.half, 0, -1):
        if step == ring.half and ring.even:
            cut = width // 2
            outs = [(0, 0, cut), (0, cut, width)]
            going = add([step], [[]], outs, beside)
        else:
            cut = 0
            outs = [(0, 0, width), (1, 0, width)]
            going = add([step, -step], [right, left], outs, beside)
        right = [(lax.ppermute(going[0], RING, ring.shift(1)), 0)]
        left = [(lax.ppermute(going[1], RING, ring.shift(-1)), cut)]
        beside = []
        for one in packed.values():
            if len(one) == 1:
                one += other_core(ring, after(one, *going))
        if step == ring.half:
            late = exchange(after(late, *going), "gx")
            if out_cuts:
                beside = w_out_piece(*going)
            beside = [beside, late, list(tokens.held.values())]
            tokens.step(*going)
            if order[0][-1] in tokens.held:
                beside = [beside, pack(0, *going)]
        if 0 not in sums and step <= ring.half - (1 if beside or step < ring.half else 0):
            while tokens.done < ring.half:
                tokens.step(*going)
            mine, theirs = in_grad_chunk(0, list(zip(early, late)), *going, list(packed.values()))
            last = pack(1, *going, pres[0])
            swap_sums(0, mine, after(theirs, right, left, last))
            beside = [pres[0]]
        elif step < ring.half and in_cuts and len(packed) == len(order):
            beside = w_in_piece(*going)
    while tokens.done < ring.half:
        tokens.step()
    for number, offsets in enumerate(order):
        if number not in packed:
            pack(number)
        if len(packed[number]) == 1:
            packed[number] += other_core(ring, packed[number])
    while out_cuts:
        w_out_piece()
    while in_cuts:
        w_in_piece()
    (in_grad,) = add([0], [right + left], [(0, 0, width)])
    return (in_grad, w_in_grad[0], w_out_grad[0])


def solution(mesh):
    placed = (
        P(("gy", "gz"), "gx"),
        P("gx", ("gy", "gz")),
        P(("gy", "gz"), "gx"),
        P("gx", ("gy", "gz")),
        P(("gy", "gz"), "gx"),
    )
    return jax.shard_map(
        shards,
        mesh=mesh,
        in_specs=placed,
        out_specs=(P(("gy", "gz"), "gx"), P("gx", ("gy", "gz")), P(("gy", "gz"), "gx")),
        check_vma=False,
    )
```

```python
import math

import jax
import jax.numpy as jnp
from jax import lax
from jax.experimental import pallas as pl
from jax.experimental.pallas import tpu as pltpu
from jax.sharding import PartitionSpec as P

RING = ("gy", "gz")


class Ring:
    def __init__(self, gy, gz):
        self.cores = 2 if gy % 2 == 0 else 1
        chips = []
        for x in range(gy // self.cores):
            line = range(gz) if x % 2 == 0 else reversed(range(gz))
            chips += [(x, z) for z in line]
        self.size, self.line = len(chips), gz
        self.half = self.size // 2
        self.even = self.size % 2 == 0
        self.rank = [
            [(x * self.cores + core) * gz + z for core in range(self.cores)] for x, z in chips
        ]

    def place(self, x, z):
        return x * self.line + jnp.where(x % 2 == 0, z, self.line - 1 - z)

    def rank_at(self, place, core):
        x, z = place // self.line, place % self.line
        return (x * 2 + core) * self.line + jnp.where(x % 2 == 0, z, self.line - 1 - z)

    def shift(self, by):
        pairs = []
        for place in range(self.size):
            target = (place + by) % self.size
            for core in range(self.cores):
                pairs.append((self.rank[place][core], self.rank[target][core]))
        return pairs

    def swap(self):
        return [(ranks[core], ranks[1 - core]) for ranks in self.rank for core in range(2)]

    def groups(self):
        cut = max(self.half - 1, 1)
        return [list(range(cut)), list(range(cut, self.half + 1))]

    def offsets(self, step):
        if step == 0:
            return [0]
        if step == self.half and self.even:
            return [self.half]
        return [-step, step]


def gelu_parts(values):
    normal_cdf = 0.5 * (1.0 + lax.erf(values / math.sqrt(2.0)))
    activity = values * normal_cdf
    slope = normal_cdf + values * jnp.exp(-0.5 * values * values) / math.sqrt(2.0 * math.pi)
    return (activity, slope)


def right_trans(left, right):
    return lax.dot_general(
        left, right, (((1,), (1,)), ((), ())), preferred_element_type=jnp.float32
    )


def left_trans(left, right):
    return lax.dot_general(
        left, right, (((0,), (0,)), ((), ())), preferred_element_type=jnp.float32
    )


VMEM = pl.BlockSpec(memory_space=pltpu.VMEM)
SMEM = pl.BlockSpec(memory_space=pltpu.SMEM)
MIB = 1 << 20


def shape(rows, columns, dtype=jnp.bfloat16):
    return jax.ShapeDtypeStruct((rows, columns), dtype)


def in_hbm(rows, columns, dtype=jnp.bfloat16):
    return pltpu.HBM((rows, columns), dtype)


def constrained(arrays):
    return [pltpu.with_memory_space_constraint(each, pltpu.HBM) for each in arrays]


def cost(flops, moved, exps=0):
    return pl.CostEstimate(flops=flops, bytes_accessed=moved, transcendentals=exps)


def tile_of(total, most):
    for tile in range(most, 127, -128):
        if total % tile == 0:
            return tile
    return total


def gelu_call(ring, pres, offsets, rows):
    held, hidden = pres[0].shape
    many, count = sum(each.shape[0] for each in pres) // held, 2 * len(offsets)

    def kernel(*refs):
        given, (act_ref, slope_ref, wide) = refs[:-3], refs[-3:]
        at = 0
        for ref in given:
            wide[at : at + ref.shape[0], :] = ref[...].astype(jnp.float32)
            at += ref.shape[0]
        me, gy = lax.axis_index("gx"), lax.axis_index("gy")
        place = ring.place(gy // 2, lax.axis_index("gz"))
        for block in range(count):
            which, offset = divmod(block, len(offsets))
            there = (place + offsets[offset] + ring.size) % ring.size
            rank = ring.rank_at(there, (gy + which) % 2)
            slot = (me - rank * rows // held + many) % many
            at = pl.multiple_of(slot * held + rank * rows % held, 8)
            activity, slope = gelu_parts(wide[pl.ds(at, rows), :])
            act_ref[block * rows : (block + 1) * rows, :] = activity.astype(act_ref.dtype)
            slope_ref[block * rows : (block + 1) * rows, :] = slope

    return pl.pallas_call(
        kernel,
        grid=(1,),
        in_specs=[VMEM] * len(pres),
        out_specs=[whole(count * rows, hidden)] * 2,
        out_shape=[in_hbm(count * rows, hidden), in_hbm(count * rows, hidden, jnp.float32)],
        scratch_shapes=[pltpu.VMEM((many * held, hidden), jnp.float32)],
        cost_estimate=cost(6000 * count * rows * hidden, 1),
        compiler_params=pltpu.CompilerParams(vmem_limit_bytes=10 * MIB),
        name="gelu",
    )(*pres)


def hold_call(weights):
    rows = weights.shape[0]
    cut = rows // 4
    weights = pltpu.with_memory_space_constraint(weights, pltpu.HBM)

    def kernel(weight_ref, out_ref, here_ref, sems):
        here_ref[...] = jnp.zeros_like(here_ref)
        copies = [
            pltpu.make_async_copy(
                weight_ref.at[pl.ds(i * cut, cut)], out_ref.at[pl.ds(i * cut, cut)], sems.at[i]
            )
            for i in range(4)
        ]
        for copy in copies:
            copy.start()
        for copy in copies:
            copy.wait()

    return pl.pallas_call(
        kernel,
        in_specs=[pl.BlockSpec(memory_space=pl.ANY)],
        out_specs=[VMEM] * 2,
        out_shape=[pltpu.VMEM(weights.shape, weights.dtype), shape(8, 128, jnp.float32)],
        scratch_shapes=[pltpu.SemaphoreType.DMA((4,))],
        cost_estimate=cost(1, 1),
        compiler_params=pltpu.CompilerParams(vmem_limit_bytes=10 * MIB),
        name="hold",
    )(weights)


def whole(rows, columns):
    return pl.BlockSpec((rows, columns), lambda i: (0, 0), pipeline_mode=pl.Buffered(1))


def split_call(left, right, cut):
    def kernel(left_ref, right_ref, low_ref, high_ref):
        low_ref[...] = left_ref[:, :cut]
        high_ref[...] = right_ref[:, cut:]

    rows, width = left.shape
    return pl.pallas_call(
        kernel,
        in_specs=[VMEM] * 2,
        out_specs=[VMEM] * 2,
        out_shape=[shape(rows, cut), shape(rows, width - cut)],
        cost_estimate=cost(1, 1),
        compiler_params=pltpu.CompilerParams(vmem_limit_bytes=10 * MIB),
        name="split",
    )(left, right)


def parts_call(values):
    rows, width = values.shape
    cut = rows * 7 // 20 // 16 * 16

    def kernel(ref, upper_ref, lower_ref):
        upper_ref[...] = ref[:cut, :]
        lower_ref[...] = ref[cut:, :]

    return pl.pallas_call(
        kernel,
        in_specs=[VMEM],
        out_specs=[VMEM] * 2,
        out_shape=[shape(cut, width), shape(rows - cut, width)],
        cost_estimate=cost(1, 1),
        compiler_params=pltpu.CompilerParams(vmem_limit_bytes=10 * MIB),
        name="parts",
    )(values)


def pack_call(blocks, rows, width, space):
    flat = [piece for block in blocks for piece in block]

    def kernel(*refs):
        given, out_ref = iter(refs), refs[-1]
        for i, block in enumerate(blocks):
            at = 0
            for piece in block:
                size = piece.shape[1]
                out_ref[i * rows : (i + 1) * rows, at : at + size] = next(given)[...]
                at += size

    return pl.pallas_call(
        kernel,
        grid=(1,),
        in_specs=[VMEM] * len(flat),
        out_specs=whole(len(blocks) * rows, width) if space is pltpu.HBM else VMEM,
        out_shape=space((len(blocks) * rows, width), jnp.bfloat16),
        cost_estimate=cost(1, 1),
        compiler_params=pltpu.CompilerParams(vmem_limit_bytes=8 * MIB),
        name="pack",
    )(*flat)


def add_call(parts, arrived, rows, outs):
    width = parts[0][0].shape[1]
    flat = [each for part in parts for each in part[:2]]
    flat += [value for block in arrived for value, _ in block]

    def kernel(*refs):
        given = iter(refs[2 * len(parts) :])
        made = refs[len(refs) - len(parts) :]
        for i, ((_, _, one, other), block) in enumerate(zip(parts, arrived)):
            mine, theirs = refs[2 * i], refs[2 * i + 1]
            low = theirs[other * rows : (other + 1) * rows, :]
            made[i][...] = mine[one * rows : (one + 1) * rows, :] + low.astype(jnp.float32)
            for value, first in block:
                columns = slice(first, first + value.shape[1])
                made[i][:, columns] += next(given)[...].astype(jnp.float32)
        for ref, (i, first, last) in zip(refs[len(flat) :], outs):
            ref[...] = made[i][:, first:last].astype(ref.dtype)

    return pl.pallas_call(
        kernel,
        in_specs=[VMEM] * len(flat),
        out_specs=[VMEM] * len(outs),
        out_shape=[shape(rows, last - first) for _, first, last in outs],
        scratch_shapes=[pltpu.VMEM((rows, width), jnp.float32)] * len(parts),
        cost_estimate=cost(1, 1),
        compiler_params=pltpu.CompilerParams(vmem_limit_bytes=8 * MIB),
        name="add",
    )(*flat)


def grad_act_call(blocks, weights, rows, cuts):
    hidden, width = weights.shape
    flat = [piece for block in blocks for piece in block]
    count = len(blocks) * rows
    tile = tile_of(hidden, 256)
    steps = hidden // tile
    spans = list(zip([0] + cuts, cuts + [count]))

    def kernel(*refs):
        weight_ref, chunk_ref, part_ref, *low_refs, joined, sem = refs[len(flat) :]
        i = pl.program_id(0)
        copy = pltpu.make_async_copy(joined, chunk_ref, sem)

        @pl.when(i == 0)
        def _():
            given = iter(refs)
            for j, block in enumerate(blocks):
                at = 0
                for piece in block:
                    size = piece.shape[1]
                    joined[j * rows : (j + 1) * rows, at : at + size] = next(given)[...]
                    at += size
            copy.start()

        at = pl.ds(pl.multiple_of(i * tile, tile), tile)
        got = right_trans(joined[...], weight_ref[at, :])
        part_ref[...] = got
        for ref, (begin, end) in zip(low_refs, spans):
            ref[...] = got[begin:end].astype(ref.dtype)

        @pl.when(i == steps - 1)
        def _():
            copy.wait()

    return pl.pallas_call(
        kernel,
        grid=(steps,),
        in_specs=[VMEM] * (len(flat) + 1),
        out_specs=[
            pl.BlockSpec(memory_space=pl.ANY),
            pl.BlockSpec((count, tile), lambda i: (0, i)),
        ]
        + [pl.BlockSpec((end - begin, tile), lambda i: (0, i)) for begin, end in spans],
        out_shape=[in_hbm(count, width), in_hbm(count, hidden, jnp.float32)]
        + [(in_hbm if begin > 0 else shape)(end - begin, hidden) for begin, end in spans],
        scratch_shapes=[pltpu.VMEM((count, width), jnp.bfloat16), pltpu.SemaphoreType.DMA],
        cost_estimate=cost(1, 1),
        compiler_params=pltpu.CompilerParams(vmem_limit_bytes=10 * MIB),
        name="grad_act",
    )(*flat, weights)


def in_grad_call(part, others, slope, weights, cuts):
    flat = [piece for pieces in zip(*others) for piece in pieces]
    width, hidden = weights.shape
    count = part.shape[0]
    half = count // 2
    tile = tile_of(width, 1024)
    spans = list(zip([0] + cuts, cuts + [half]))

    def kernel(*refs):
        part_ref, slope_ref = refs[:2]
        weight_ref, pre_ref, mine_ref, *theirs_refs = refs[2 + len(flat) :]
        i = pl.program_id(0)

        @pl.when(i == 0)
        def _():
            given, at = iter(refs[2:]), 0
            for pieces in zip(*others):
                here = slice(at, at + pieces[0].shape[0])
                total = part_ref[here, :]
                for _ in pieces:
                    total = total + next(given)[...].astype(jnp.float32)
                pre_ref[here, :] = (total * slope_ref[here, :]).astype(pre_ref.dtype)
                at = here.stop

        at = pl.ds(pl.multiple_of(i * tile, tile), tile)
        got = right_trans(pre_ref[...], weight_ref[at, :])
        mine_ref[:, at] = got[:half]
        for ref, (begin, end) in zip(theirs_refs, spans):
            ref[...] = got[half + begin : half + end].astype(ref.dtype)

    return pl.pallas_call(
        kernel,
        grid=(width // tile,),
        in_specs=[whole(count, hidden)] * 2 + [whole(*each.shape) for each in flat] + [VMEM],
        out_specs=[
            whole(count, hidden),
            VMEM,
        ]
        + [pl.BlockSpec((end - begin, tile), lambda i: (0, i)) for begin, end in spans],
        out_shape=[
            in_hbm(count, hidden),
            pltpu.VMEM((half, width), jnp.float32),
        ]
        + [shape(end - begin, width) for begin, end in spans],
        cost_estimate=cost(1, 1),
        compiler_params=pltpu.CompilerParams(vmem_limit_bytes=14 * MIB),
        name="in_grad",
    )(part, slope, *flat, weights)


def pieces_of(width, most):
    tile = tile_of(width, 1024)
    tiles = width // tile
    calls = min(most, tiles)
    ends = [tiles * i // calls for i in range(calls + 1)]
    return tile, [(first, last - first) for first, last in zip(ends, ends[1:])]


def w_out_grad_call(acts, chunks, factor, tile, first, count, earlier):
    sizes = [chunk.shape[0] for chunk in chunks]
    many, total = len(sizes), sum(sizes)
    hidden, width = earlier[0].shape if earlier else (acts[0].shape[1], chunks[0].shape[1])

    def kernel(*refs):
        given, tokens = refs[: len(acts)], refs[len(acts) : len(acts) + many]
        if earlier:
            turned, out_ref = given[0], refs[-1]
        else:
            out_ref, turned = refs[-2:]

            @pl.when(pl.program_id(0) == 0)
            def _():
                turned[...] = jnp.concatenate([ref[...] for ref in given], axis=0).T

        joined = jnp.concatenate([ref[...] for ref in tokens], axis=0)
        got = jnp.dot(turned[...], joined, preferred_element_type=jnp.float32)
        out_ref[...] = (got * factor).astype(out_ref.dtype)

    out_spec = pl.BlockSpec((hidden, tile), lambda i: (0, first + i))
    return pl.pallas_call(
        kernel,
        grid=(count,),
        in_specs=[whole(*act.shape) for act in acts]
        + [pl.BlockSpec((size, tile), lambda i: (0, first + i)) for size in sizes]
        + [pl.BlockSpec(memory_space=pl.ANY)] * len(earlier),
        out_specs=[out_spec] + ([] if earlier else [whole(hidden, total)]),
        out_shape=[shape(hidden, width)] + ([] if earlier else [shape(hidden, total)]),
        input_output_aliases={len(acts) + many: 0} if earlier else {},
        cost_estimate=cost(16 * total * tile // 4 * count * hidden, 2 * hidden * tile * count),
        compiler_params=pltpu.CompilerParams(vmem_limit_bytes=26 * MIB),
        name="w_out_grad",
    )(*acts, *chunks, *earlier)


def w_in_grad_call(blocks, pres, factor, tile, first, count, earlier):
    width = blocks[0].shape[1]
    many, sizes = len(blocks), [pre.shape[0] for pre in pres]
    total, hidden = sum(sizes), pres[0].shape[1]

    def kernel(*refs):
        given, wanted = refs[:many], refs[many : many + len(sizes)]
        out_ref, tokens, grads = refs[-3:]

        @pl.when(pl.program_id(0) == 0)
        def _():
            at = 0
            for ref, size in zip(wanted, sizes):
                grads[at : at + size, :] = ref[...]
                at += size

        at = 0
        for ref in given:
            tokens[at : at + ref.shape[0], :] = ref[...]
            at += ref.shape[0]
        got = left_trans(tokens[...], grads[...])
        out_ref[...] = (got * factor).astype(out_ref.dtype)

    return pl.pallas_call(
        kernel,
        grid=(count,),
        in_specs=[pl.BlockSpec((each.shape[0], tile), lambda i: (0, first + i)) for each in blocks]
        + [whole(size, hidden) for size in sizes]
        + [pl.BlockSpec(memory_space=pl.ANY)] * len(earlier),
        out_specs=pl.BlockSpec((tile, hidden), lambda i: (first + i, 0)),
        out_shape=shape(width, hidden),
        input_output_aliases={many + len(sizes): 0} if earlier else {},
        scratch_shapes=[
            pltpu.VMEM((total, tile), jnp.bfloat16),
            pltpu.VMEM((total, hidden), jnp.bfloat16),
        ],
        cost_estimate=cost(3 * total * tile * count * hidden, 2 * hidden * tile * count),
        compiler_params=pltpu.CompilerParams(vmem_limit_bytes=26 * MIB),
        name="w_in_grad",
    )(*blocks, *pres, *earlier)


def after(values, *others):
    return lax.optimization_barrier((values, others))[0]


class Gather:
    def __init__(self, ring, block, halve):
        self.ring, self.halve = ring, halve
        self.held = {0: [block]}
        self.left = self.right = block
        self.done = 0

    def step(self, *others):
        ring = self.ring
        self.done += 1
        left, right = self.left, self.right
        if others:
            left, right = after((left, right), *others)
        if self.done == ring.half and ring.even:
            if self.halve:
                cut = left.shape[1] // 2
                low, high = split_call(left, right, cut)
                low = lax.ppermute(low, RING, ring.shift(1))
                high = lax.ppermute(high, RING, ring.shift(-1))
                self.held[self.done] = [low, high]
            else:
                self.held[self.done] = [lax.ppermute(left, RING, ring.shift(1))]
        else:
            self.left = lax.ppermute(left, RING, ring.shift(1))
            self.right = lax.ppermute(right, RING, ring.shift(-1))
            self.held[-self.done], self.held[self.done] = [self.left], [self.right]


def other_core(ring, pieces):
    return [lax.ppermute(piece, RING, ring.swap()) for piece in pieces]


def exchange(values, axis):
    size = lax.axis_size(axis)
    return [
        lax.ppermute(values, axis, [(i, (i + by) % size) for i in range(size)])
        for by in range(1, size)
    ]


def shards(inputs, pre_act, out_grad, w_in, w_out):
    ring = Ring(lax.axis_size("gy"), lax.axis_size("gz"))
    assert ring.cores == 2
    rows, width = inputs.shape
    groups = ring.size * 2
    factor = 1.0 / math.sqrt(rows * groups)
    order = [[o for step in group for o in ring.offsets(step)] for group in ring.groups()]

    w_out, here = hold_call(w_out)
    upper, lower = parts_call(pre_act)
    came = [exchange(upper, "gx")]

    grads = Gather(ring, out_grad, True)
    chunks, partials, swapped = [], [], {0: other_core(ring, grads.held[0])}
    for number, offsets in enumerate(order):
        first, last = ring.groups()[number][0], ring.groups()[number][-1]
        while grads.done < last:
            if number > 0 and grads.done >= first:
                grads.step(sent)
            elif grads.done == 1:
                grads.step(here, came[0], swapped[0])
                came.append(exchange(after(lower, came[0], here), "gx"))
            else:
                earlier = [each for offset, each in swapped.items() if abs(offset) < grads.done]
                grads.step(*([earlier, came] if grads.done > 1 else []))
            if number > 0 and grads.done == last:
                pres_x = [pre_act] + [each for pieces in zip(*came) for each in pieces]
                ready = after(pres_x, sent)
                acts, slopes = zip(*[gelu_call(ring, ready, each, rows) for each in order])
            for offset in ring.offsets(grads.done):
                ahead = here if number == 0 else slopes if grads.done == last else sent
                swapped[offset] = other_core(ring, after(grads.held[offset], ahead))
        blocks = [grads.held[o] for o in offsets] + [swapped[o] for o in offsets]
        cuts = [len(blocks) * rows * part // 25 // 16 * 16 for part in (10, 17)] if number == 0 else []
        if number > 0:
            blocks[0] = after(blocks[0], early)
        chunk, partial, *sent = grad_act_call(blocks, w_out, rows, cuts)
        chunks.append(chunk)
        partials.append(partial)
        if number == 0:
            early, late = exchange(sent[0], "gx"), sent[1:]
    received = [[each] for each in exchange(sent[0], "gx")]

    tokens = Gather(ring, after(inputs, grads.held[ring.half], swapped), True)
    chunks = constrained(chunks)

    def advance(*others):
        arrived = list(tokens.held.values())[1:]
        if tokens.done < ring.half:
            tokens.step(*others)
        return arrived

    tile, in_cuts = pieces_of(width, 2)
    out_cuts = pieces_of(width, 6)[1]
    if len(out_cuts) == 6:
        out_cuts = [(0, 1), (1, 3), (4, 2)]
    w_out_grad, w_in_grad, turned = [], [], None

    def w_out_piece(*others):
        nonlocal w_out_grad, turned
        first, count = out_cuts.pop(0)
        given = list(acts) if turned is None else [turned]
        given[0] = after(given[0], *others)
        got = w_out_grad_call(given, chunks, factor, tile, first, count, w_out_grad)
        w_out_grad = got[:1]
        if turned is None:
            turned = got[1]
        return w_out_grad

    def w_in_piece(*others):
        nonlocal w_in_grad
        first, count = in_cuts.pop(0)
        flat = [each for number in range(len(order)) for each in packed[number]]
        given = [after(pres[0], *others)] + pres[1:]
        w_in_grad = [w_in_grad_call(flat, given, factor, tile, first, count, w_in_grad)]
        return w_in_grad

    w_out_piece(advance(), early)
    arrived = advance()
    w_in = pltpu.with_memory_space_constraint(w_in, pltpu.VMEM)
    if len(out_cuts) > 1:
        w_out_piece(arrived)

    sums, pres = {}, [None] * len(order)

    def in_grad_chunk(i, received, *others):
        partial = after(partials[i], *others)
        cuts = [(len(order[i]) - 2) * rows] if i == 0 and len(order[i]) > 2 else []
        pres[i], mine, *theirs = in_grad_call(partial, received, slopes[i], w_in, cuts)
        return mine, theirs

    def swap_sums(i, mine, theirs):
        place = len(order[i])
        for piece in reversed(theirs):
            got = lax.ppermute(piece, RING, ring.swap())
            for other in reversed(range(piece.shape[0] // rows)):
                place -= 1
                sums[order[i][place]] = (mine, got, place, other)

    def add(offsets, arrived, outs, *others):
        parts = [sums[offset] for offset in offsets]
        parts[0] = (parts[0][0], after(parts[0][1], *others)) + parts[0][2:]
        return add_call(parts, arrived, rows, outs)

    packed = {}

    def pack(number, *others):
        blocks = after([tokens.held[o] for o in order[number]], *others)
        space = pltpu.HBM if number == 0 else pltpu.VMEM
        packed[number] = [pack_call(blocks, rows, width, space)]
        return packed[number]

    mine, theirs = in_grad_chunk(1, received, w_out_grad, advance(*w_out_grad))
    middle = exchange(after(late[0], received), "gx")
    swap_sums(1, mine, after(theirs, list(tokens.held.values()), middle))
    right, left, beside = [], [], []
    for step in range(ring.half, 0, -1):
        if step == ring.half and ring.even:
            cut = width // 2
            outs = [(0, 0, cut), (0, cut, width)]
            going = add([step], [[]], outs, beside)
        else:
            cut = 0
            outs = [(0, 0, width), (1, 0, width)]
            going = add([step, -step], [right, left], outs, beside)
        right = [(lax.ppermute(going[0], RING, ring.shift(1)), 0)]
        left = [(lax.ppermute(going[1], RING, ring.shift(-1)), cut)]
        beside = []
        for one in packed.values():
            if len(one) == 1:
                one += other_core(ring, after(one, *going))
        if step == ring.half:
            late = exchange(after(late[1], middle), "gx")
            if out_cuts:
                beside = w_out_piece(*going)
            tokens.step(*going)
            beside = [beside, late, list(tokens.held.values())]
            if order[0][-1] in tokens.held:
                beside = [beside, pack(0, *going)]
        if 0 not in sums and step <= ring.half - (1 if beside or step < ring.half else 0):
            while tokens.done < ring.half:
                tokens.step(*going)
            mine, theirs = in_grad_chunk(0, list(zip(early, middle, late)), *going, list(packed.values()))
            last = pack(1, *going, pres[0])
            swap_sums(0, mine, after(theirs, right, left, last))
            beside = [pres[0]]
        elif step < ring.half and in_cuts and len(packed) == len(order):
            beside = w_in_piece(*going)
    while tokens.done < ring.half:
        tokens.step()
    for number, offsets in enumerate(order):
        if number not in packed:
            pack(number)
        if len(packed[number]) == 1:
            packed[number] += other_core(ring, packed[number])
    while out_cuts:
        w_out_piece()
    while in_cuts:
        w_in_piece()
    (in_grad,) = add([0], [right + left], [(0, 0, width)])
    return (in_grad, w_in_grad[0], w_out_grad[0])


def solution(mesh):
    placed = (
        P(("gy", "gz"), "gx"),
        P("gx", ("gy", "gz")),
        P(("gy", "gz"), "gx"),
        P("gx", ("gy", "gz")),
        P(("gy", "gz"), "gx"),
    )
    return jax.shard_map(
        shards,
        mesh=mesh,
        in_specs=placed,
        out_specs=(P(("gy", "gz"), "gx"), P("gx", ("gy", "gz")), P(("gy", "gz"), "gx")),
        check_vma=False,
    )
```

```python
import math

import jax
import jax.numpy as jnp
from jax import lax
from jax.experimental import pallas as pl
from jax.experimental.pallas import tpu as pltpu
from jax.sharding import PartitionSpec as P

RING = ("gy", "gz")


class Ring:
    def __init__(self, gy, gz):
        self.cores = 2 if gy % 2 == 0 else 1
        chips = []
        for x in range(gy // self.cores):
            line = range(gz) if x % 2 == 0 else reversed(range(gz))
            chips += [(x, z) for z in line]
        self.size, self.line = len(chips), gz
        self.half = self.size // 2
        self.even = self.size % 2 == 0
        self.rank = [
            [(x * self.cores + core) * gz + z for core in range(self.cores)] for x, z in chips
        ]

    def place(self, x, z):
        return x * self.line + jnp.where(x % 2 == 0, z, self.line - 1 - z)

    def rank_at(self, place, core):
        x, z = place // self.line, place % self.line
        return (x * 2 + core) * self.line + jnp.where(x % 2 == 0, z, self.line - 1 - z)

    def shift(self, by):
        pairs = []
        for place in range(self.size):
            target = (place + by) % self.size
            for core in range(self.cores):
                pairs.append((self.rank[place][core], self.rank[target][core]))
        return pairs

    def swap(self):
        return [(ranks[core], ranks[1 - core]) for ranks in self.rank for core in range(2)]

    def groups(self):
        cut = max(self.half - 1, 1)
        return [list(range(cut)), list(range(cut, self.half + 1))]

    def offsets(self, step):
        if step == 0:
            return [0]
        if step == self.half and self.even:
            return [self.half]
        return [-step, step]


def gelu_parts(values):
    normal_cdf = 0.5 * (1.0 + lax.erf(values / math.sqrt(2.0)))
    activity = values * normal_cdf
    slope = normal_cdf + values * jnp.exp(-0.5 * values * values) / math.sqrt(2.0 * math.pi)
    return (activity, slope)


def right_trans(left, right):
    return lax.dot_general(
        left, right, (((1,), (1,)), ((), ())), preferred_element_type=jnp.float32
    )


def left_trans(left, right):
    return lax.dot_general(
        left, right, (((0,), (0,)), ((), ())), preferred_element_type=jnp.float32
    )


VMEM = pl.BlockSpec(memory_space=pltpu.VMEM)
SMEM = pl.BlockSpec(memory_space=pltpu.SMEM)
MIB = 1 << 20


def shape(rows, columns, dtype=jnp.bfloat16):
    return jax.ShapeDtypeStruct((rows, columns), dtype)


def in_hbm(rows, columns, dtype=jnp.bfloat16):
    return pltpu.HBM((rows, columns), dtype)


def constrained(arrays):
    return [pltpu.with_memory_space_constraint(each, pltpu.HBM) for each in arrays]


def cost(flops, moved, exps=0):
    return pl.CostEstimate(flops=flops, bytes_accessed=moved, transcendentals=exps)


def tile_of(total, most):
    for tile in range(most, 127, -128):
        if total % tile == 0:
            return tile
    return total


def gelu_call(ring, pres, offsets, rows):
    held, hidden = pres[0].shape
    many, count = sum(each.shape[0] for each in pres) // held, 2 * len(offsets)

    def kernel(*refs):
        given, (act_ref, slope_ref, wide) = refs[:-3], refs[-3:]
        at = 0
        for ref in given:
            wide[at : at + ref.shape[0], :] = ref[...].astype(jnp.float32)
            at += ref.shape[0]
        me, gy = lax.axis_index("gx"), lax.axis_index("gy")
        place = ring.place(gy // 2, lax.axis_index("gz"))
        for block in range(count):
            which, offset = divmod(block, len(offsets))
            there = (place + offsets[offset] + ring.size) % ring.size
            rank = ring.rank_at(there, (gy + which) % 2)
            slot = (me - rank * rows // held + many) % many
            at = pl.multiple_of(slot * held + rank * rows % held, 8)
            activity, slope = gelu_parts(wide[pl.ds(at, rows), :])
            act_ref[block * rows : (block + 1) * rows, :] = activity.astype(act_ref.dtype)
            slope_ref[block * rows : (block + 1) * rows, :] = slope

    return pl.pallas_call(
        kernel,
        grid=(1,),
        in_specs=[VMEM] * len(pres),
        out_specs=[whole(count * rows, hidden)] * 2,
        out_shape=[in_hbm(count * rows, hidden), in_hbm(count * rows, hidden, jnp.float32)],
        scratch_shapes=[pltpu.VMEM((many * held, hidden), jnp.float32)],
        cost_estimate=cost(6000 * count * rows * hidden, 1),
        compiler_params=pltpu.CompilerParams(vmem_limit_bytes=10 * MIB),
        name="gelu",
    )(*pres)


def hold_call(weights):
    rows = weights.shape[0]
    cut = rows // 4
    weights = pltpu.with_memory_space_constraint(weights, pltpu.HBM)

    def kernel(weight_ref, out_ref, here_ref, sems):
        here_ref[...] = jnp.zeros_like(here_ref)
        copies = [
            pltpu.make_async_copy(
                weight_ref.at[pl.ds(i * cut, cut)], out_ref.at[pl.ds(i * cut, cut)], sems.at[i]
            )
            for i in range(4)
        ]
        for copy in copies:
            copy.start()
        for copy in copies:
            copy.wait()

    return pl.pallas_call(
        kernel,
        in_specs=[pl.BlockSpec(memory_space=pl.ANY)],
        out_specs=[VMEM] * 2,
        out_shape=[pltpu.VMEM(weights.shape, weights.dtype), shape(8, 128, jnp.float32)],
        scratch_shapes=[pltpu.SemaphoreType.DMA((4,))],
        cost_estimate=cost(1, 1),
        compiler_params=pltpu.CompilerParams(vmem_limit_bytes=10 * MIB),
        name="hold",
    )(weights)


def whole(rows, columns):
    return pl.BlockSpec((rows, columns), lambda i: (0, 0), pipeline_mode=pl.Buffered(1))


def split_call(left, right, cut):
    def kernel(left_ref, right_ref, low_ref, high_ref):
        low_ref[...] = left_ref[:, :cut]
        high_ref[...] = right_ref[:, cut:]

    rows, width = left.shape
    return pl.pallas_call(
        kernel,
        in_specs=[VMEM] * 2,
        out_specs=[VMEM] * 2,
        out_shape=[shape(rows, cut), shape(rows, width - cut)],
        cost_estimate=cost(1, 1),
        compiler_params=pltpu.CompilerParams(vmem_limit_bytes=10 * MIB),
        name="split",
    )(left, right)


def parts_call(values):
    rows, width = values.shape
    cut = rows // 2 // 16 * 16

    def kernel(ref, upper_ref, lower_ref):
        upper_ref[...] = ref[:cut, :]
        lower_ref[...] = ref[cut:, :]

    return pl.pallas_call(
        kernel,
        in_specs=[VMEM],
        out_specs=[VMEM] * 2,
        out_shape=[shape(cut, width), shape(rows - cut, width)],
        cost_estimate=cost(1, 1),
        compiler_params=pltpu.CompilerParams(vmem_limit_bytes=10 * MIB),
        name="parts",
    )(values)


def pack_call(blocks, rows, width, space):
    flat = [piece for block in blocks for piece in block]

    def kernel(*refs):
        given, out_ref = iter(refs), refs[-1]
        for i, block in enumerate(blocks):
            at = 0
            for piece in block:
                size = piece.shape[1]
                out_ref[i * rows : (i + 1) * rows, at : at + size] = next(given)[...]
                at += size

    return pl.pallas_call(
        kernel,
        grid=(1,),
        in_specs=[VMEM] * len(flat),
        out_specs=whole(len(blocks) * rows, width) if space is pltpu.HBM else VMEM,
        out_shape=space((len(blocks) * rows, width), jnp.bfloat16),
        cost_estimate=cost(1, 1),
        compiler_params=pltpu.CompilerParams(vmem_limit_bytes=8 * MIB),
        name="pack",
    )(*flat)


def add_call(parts, arrived, rows, outs):
    width = parts[0][0].shape[1]
    flat = [each for part in parts for each in part[:2]]
    flat += [value for block in arrived for value, _ in block]

    def kernel(*refs):
        given = iter(refs[2 * len(parts) :])
        made = refs[len(refs) - len(parts) :]
        for i, ((_, _, one, other), block) in enumerate(zip(parts, arrived)):
            mine, theirs = refs[2 * i], refs[2 * i + 1]
            low = theirs[other * rows : (other + 1) * rows, :]
            made[i][...] = mine[one * rows : (one + 1) * rows, :] + low.astype(jnp.float32)
            for value, first in block:
                columns = slice(first, first + value.shape[1])
                made[i][:, columns] += next(given)[...].astype(jnp.float32)
        for ref, (i, first, last) in zip(refs[len(flat) :], outs):
            ref[...] = made[i][:, first:last].astype(ref.dtype)

    return pl.pallas_call(
        kernel,
        in_specs=[VMEM] * len(flat),
        out_specs=[VMEM] * len(outs),
        out_shape=[shape(rows, last - first) for _, first, last in outs],
        scratch_shapes=[pltpu.VMEM((rows, width), jnp.float32)] * len(parts),
        cost_estimate=cost(1, 1),
        compiler_params=pltpu.CompilerParams(vmem_limit_bytes=8 * MIB),
        name="add",
    )(*flat)


def grad_act_call(blocks, weights, rows, cuts):
    hidden, width = weights.shape
    flat = [piece for block in blocks for piece in block]
    count = len(blocks) * rows
    tile = tile_of(hidden, 256)
    steps = hidden // tile
    spans = list(zip([0] + cuts, cuts + [count]))

    def kernel(*refs):
        weight_ref, chunk_ref, part_ref, *low_refs, joined, sem = refs[len(flat) :]
        i = pl.program_id(0)
        copy = pltpu.make_async_copy(joined, chunk_ref, sem)

        @pl.when(i == 0)
        def _():
            given = iter(refs)
            for j, block in enumerate(blocks):
                at = 0
                for piece in block:
                    size = piece.shape[1]
                    joined[j * rows : (j + 1) * rows, at : at + size] = next(given)[...]
                    at += size
            copy.start()

        at = pl.ds(pl.multiple_of(i * tile, tile), tile)
        got = right_trans(joined[...], weight_ref[at, :])
        part_ref[...] = got
        for ref, (begin, end) in zip(low_refs, spans):
            ref[...] = got[begin:end].astype(ref.dtype)

        @pl.when(i == steps - 1)
        def _():
            copy.wait()

    return pl.pallas_call(
        kernel,
        grid=(steps,),
        in_specs=[VMEM] * (len(flat) + 1),
        out_specs=[
            pl.BlockSpec(memory_space=pl.ANY),
            pl.BlockSpec((count, tile), lambda i: (0, i)),
        ]
        + [pl.BlockSpec((end - begin, tile), lambda i: (0, i)) for begin, end in spans],
        out_shape=[in_hbm(count, width), in_hbm(count, hidden, jnp.float32)]
        + [(in_hbm if begin > 0 else shape)(end - begin, hidden) for begin, end in spans],
        scratch_shapes=[pltpu.VMEM((count, width), jnp.bfloat16), pltpu.SemaphoreType.DMA],
        cost_estimate=cost(1, 1),
        compiler_params=pltpu.CompilerParams(vmem_limit_bytes=10 * MIB),
        name="grad_act",
    )(*flat, weights)


def in_grad_call(part, others, slope, weights, cuts):
    flat = [piece for pieces in zip(*others) for piece in pieces]
    width, hidden = weights.shape
    count = part.shape[0]
    half = count // 2
    tile = tile_of(width, 1024)
    spans = list(zip([0] + cuts, cuts + [half]))

    def kernel(*refs):
        part_ref, slope_ref = refs[:2]
        weight_ref, pre_ref, mine_ref, *theirs_refs = refs[2 + len(flat) :]
        i = pl.program_id(0)

        @pl.when(i == 0)
        def _():
            given, at = iter(refs[2:]), 0
            for pieces in zip(*others):
                here = slice(at, at + pieces[0].shape[0])
                total = part_ref[here, :]
                for _ in pieces:
                    total = total + next(given)[...].astype(jnp.float32)
                pre_ref[here, :] = (total * slope_ref[here, :]).astype(pre_ref.dtype)
                at = here.stop

        at = pl.ds(pl.multiple_of(i * tile, tile), tile)
        got = right_trans(pre_ref[...], weight_ref[at, :])
        mine_ref[:, at] = got[:half]
        for ref, (begin, end) in zip(theirs_refs, spans):
            ref[...] = got[half + begin : half + end].astype(ref.dtype)

    return pl.pallas_call(
        kernel,
        grid=(width // tile,),
        in_specs=[whole(count, hidden)] * 2 + [whole(*each.shape) for each in flat] + [VMEM],
        out_specs=[
            whole(count, hidden),
            VMEM,
        ]
        + [pl.BlockSpec((end - begin, tile), lambda i: (0, i)) for begin, end in spans],
        out_shape=[
            in_hbm(count, hidden),
            pltpu.VMEM((half, width), jnp.float32),
        ]
        + [shape(end - begin, width) for begin, end in spans],
        cost_estimate=cost(1, 1),
        compiler_params=pltpu.CompilerParams(vmem_limit_bytes=14 * MIB),
        name="in_grad",
    )(part, slope, *flat, weights)


def pieces_of(width, most):
    tile = tile_of(width, 1024)
    tiles = width // tile
    calls = min(most, tiles)
    ends = [tiles * i // calls for i in range(calls + 1)]
    return tile, [(first, last - first) for first, last in zip(ends, ends[1:])]


def w_out_grad_call(acts, chunks, factor, tile, first, count, earlier):
    sizes = [chunk.shape[0] for chunk in chunks]
    many, total = len(sizes), sum(sizes)
    hidden, width = earlier[0].shape if earlier else (acts[0].shape[1], chunks[0].shape[1])

    def kernel(*refs):
        given, tokens = refs[: len(acts)], refs[len(acts) : len(acts) + many]
        if earlier:
            turned, out_ref = given[0], refs[-1]
        else:
            out_ref, turned = refs[-2:]

            @pl.when(pl.program_id(0) == 0)
            def _():
                turned[...] = jnp.concatenate([ref[...] for ref in given], axis=0).T

        joined = jnp.concatenate([ref[...] for ref in tokens], axis=0)
        got = jnp.dot(turned[...], joined, preferred_element_type=jnp.float32)
        out_ref[...] = (got * factor).astype(out_ref.dtype)

    out_spec = pl.BlockSpec((hidden, tile), lambda i: (0, first + i))
    return pl.pallas_call(
        kernel,
        grid=(count,),
        in_specs=[whole(*act.shape) for act in acts]
        + [pl.BlockSpec((size, tile), lambda i: (0, first + i)) for size in sizes]
        + [pl.BlockSpec(memory_space=pl.ANY)] * len(earlier),
        out_specs=[out_spec] + ([] if earlier else [whole(hidden, total)]),
        out_shape=[shape(hidden, width)] + ([] if earlier else [shape(hidden, total)]),
        input_output_aliases={len(acts) + many: 0} if earlier else {},
        cost_estimate=cost(16 * total * tile // 4 * count * hidden, 2 * hidden * tile * count),
        compiler_params=pltpu.CompilerParams(vmem_limit_bytes=26 * MIB),
        name="w_out_grad",
    )(*acts, *chunks, *earlier)


def w_in_grad_call(blocks, pres, factor, tile, first, count, earlier):
    width = blocks[0].shape[1]
    many, sizes = len(blocks), [pre.shape[0] for pre in pres]
    total, hidden = sum(sizes), pres[0].shape[1]

    def kernel(*refs):
        given, wanted = refs[:many], refs[many : many + len(sizes)]
        out_ref, tokens, grads = refs[-3:]

        @pl.when(pl.program_id(0) == 0)
        def _():
            at = 0
            for ref, size in zip(wanted, sizes):
                grads[at : at + size, :] = ref[...]
                at += size

        at = 0
        for ref in given:
            tokens[at : at + ref.shape[0], :] = ref[...]
            at += ref.shape[0]
        got = left_trans(tokens[...], grads[...])
        out_ref[...] = (got * factor).astype(out_ref.dtype)

    return pl.pallas_call(
        kernel,
        grid=(count,),
        in_specs=[pl.BlockSpec((each.shape[0], tile), lambda i: (0, first + i)) for each in blocks]
        + [whole(size, hidden) for size in sizes]
        + [pl.BlockSpec(memory_space=pl.ANY)] * len(earlier),
        out_specs=pl.BlockSpec((tile, hidden), lambda i: (first + i, 0)),
        out_shape=shape(width, hidden),
        input_output_aliases={many + len(sizes): 0} if earlier else {},
        scratch_shapes=[
            pltpu.VMEM((total, tile), jnp.bfloat16),
            pltpu.VMEM((total, hidden), jnp.bfloat16),
        ],
        cost_estimate=cost(3 * total * tile * count * hidden, 2 * hidden * tile * count),
        compiler_params=pltpu.CompilerParams(vmem_limit_bytes=26 * MIB),
        name="w_in_grad",
    )(*blocks, *pres, *earlier)


def after(values, *others):
    return lax.optimization_barrier((values, others))[0]


class Gather:
    def __init__(self, ring, block, halve):
        self.ring, self.halve = ring, halve
        self.held = {0: [block]}
        self.left = self.right = block
        self.done = 0

    def step(self, *others):
        ring = self.ring
        self.done += 1
        left, right = self.left, self.right
        if others:
            left, right = after((left, right), *others)
        if self.done == ring.half and ring.even:
            if self.halve:
                cut = left.shape[1] // 2
                low, high = split_call(left, right, cut)
                low = lax.ppermute(low, RING, ring.shift(1))
                high = lax.ppermute(high, RING, ring.shift(-1))
                self.held[self.done] = [low, high]
            else:
                self.held[self.done] = [lax.ppermute(left, RING, ring.shift(1))]
        else:
            self.left = lax.ppermute(left, RING, ring.shift(1))
            self.right = lax.ppermute(right, RING, ring.shift(-1))
            self.held[-self.done], self.held[self.done] = [self.left], [self.right]


def other_core(ring, pieces):
    return [lax.ppermute(piece, RING, ring.swap()) for piece in pieces]


def exchange(values, axis):
    size = lax.axis_size(axis)
    return [
        lax.ppermute(values, axis, [(i, (i + by) % size) for i in range(size)])
        for by in range(1, size)
    ]


def shards(inputs, pre_act, out_grad, w_in, w_out):
    ring = Ring(lax.axis_size("gy"), lax.axis_size("gz"))
    assert ring.cores == 2
    rows, width = inputs.shape
    groups = ring.size * 2
    factor = 1.0 / math.sqrt(rows * groups)
    order = [[o for step in group for o in ring.offsets(step)] for group in ring.groups()]

    w_out, here = hold_call(w_out)
    upper, lower = parts_call(pre_act)
    came = [exchange(upper, "gx")]

    grads = Gather(ring, out_grad, True)
    chunks, partials, swapped = [], [], {0: other_core(ring, grads.held[0])}
    for number, offsets in enumerate(order):
        first, last = ring.groups()[number][0], ring.groups()[number][-1]
        while grads.done < last:
            if number > 0 and grads.done >= first:
                grads.step(sent, came)
            elif grads.done == 1:
                grads.step(here, swapped[0])
                came.append(exchange(after(lower, came[0], grads.held[1]), "gx"))
            else:
                earlier = [each for offset, each in swapped.items() if abs(offset) < grads.done]
                grads.step(*([earlier, came[0]] if grads.done > 1 else []))
            if number > 0 and grads.done == last:
                pres_x = [pre_act] + [each for pieces in zip(*came) for each in pieces]
                ready = after(pres_x, sent)
                acts, slopes = zip(*[gelu_call(ring, ready, each, rows) for each in order])
            for offset in ring.offsets(grads.done):
                ahead = here if number == 0 else slopes if grads.done == last else sent
                swapped[offset] = other_core(ring, after(grads.held[offset], ahead))
        blocks = [grads.held[o] for o in offsets] + [swapped[o] for o in offsets]
        cuts = [len(blocks) * rows * part // 25 // 16 * 16 for part in (10, 17)] if number == 0 else []
        if number > 0:
            blocks[0] = after(blocks[0], early)
        chunk, partial, *sent = grad_act_call(blocks, w_out, rows, cuts)
        chunks.append(chunk)
        partials.append(partial)
        if number == 0:
            early, late = exchange(sent[0], "gx"), sent[1:]
    received = [[each] for each in exchange(sent[0], "gx")]

    tokens = Gather(ring, after(inputs, grads.held[ring.half], [each for offset, each in swapped.items() if offset != ring.half]), True)
    chunks = constrained(chunks)

    def advance(*others):
        arrived = list(tokens.held.values())[1:]
        if tokens.done < ring.half:
            tokens.step(*others)
        return arrived

    tile, in_cuts = pieces_of(width, 2)
    out_cuts = pieces_of(width, 6)[1]
    if len(out_cuts) == 6:
        out_cuts = [(0, 1), (1, 3), (4, 2)]
    w_out_grad, w_in_grad, turned = [], [], None

    def w_out_piece(*others):
        nonlocal w_out_grad, turned
        first, count = out_cuts.pop(0)
        given = list(acts) if turned is None else [turned]
        given[0] = after(given[0], *others)
        got = w_out_grad_call(given, chunks, factor, tile, first, count, w_out_grad)
        w_out_grad = got[:1]
        if turned is None:
            turned = got[1]
        return w_out_grad

    def w_in_piece(*others):
        nonlocal w_in_grad
        first, count = in_cuts.pop(0)
        flat = [each for number in range(len(order)) for each in packed[number]]
        given = [after(pres[0], *others)] + pres[1:]
        w_in_grad = [w_in_grad_call(flat, given, factor, tile, first, count, w_in_grad)]
        return w_in_grad

    w_out_piece(advance(), early)
    arrived = advance()
    w_in = pltpu.with_memory_space_constraint(w_in, pltpu.VMEM)
    if len(out_cuts) > 1:
        w_out_piece(arrived)

    sums, pres = {}, [None] * len(order)

    def in_grad_chunk(i, received, *others):
        partial = after(partials[i], *others)
        cuts = [(len(order[i]) - 2) * rows] if i == 0 and len(order[i]) > 2 else []
        pres[i], mine, *theirs = in_grad_call(partial, received, slopes[i], w_in, cuts)
        return mine, theirs

    def swap_sums(i, mine, theirs):
        place = len(order[i])
        for piece in reversed(theirs):
            got = lax.ppermute(piece, RING, ring.swap())
            for other in reversed(range(piece.shape[0] // rows)):
                place -= 1
                sums[order[i][place]] = (mine, got, place, other)

    def add(offsets, arrived, outs, *others):
        parts = [sums[offset] for offset in offsets]
        parts[0] = (parts[0][0], after(parts[0][1], *others)) + parts[0][2:]
        return add_call(parts, arrived, rows, outs)

    packed = {}

    def pack(number, *others):
        blocks = after([tokens.held[o] for o in order[number]], *others)
        space = pltpu.HBM if number == 0 else pltpu.VMEM
        packed[number] = [pack_call(blocks, rows, width, space)]
        return packed[number]

    mine, theirs = in_grad_chunk(1, received, w_out_grad, advance(*w_out_grad))
    middle = exchange(after(late[0], received), "gx")
    if order[0][-1] in tokens.held:
        pack(0, pres[1])
    swap_sums(1, mine, after(theirs, list(tokens.held.values()), middle, list(packed.values())))
    right, left, beside = [], [], []
    for step in range(ring.half, 0, -1):
        if step == ring.half and ring.even:
            cut = width // 2
            outs = [(0, 0, cut), (0, cut, width)]
            going = add([step], [[]], outs, beside)
        else:
            cut = 0
            outs = [(0, 0, width), (1, 0, width)]
            going = add([step, -step], [right, left], outs, beside)
        right = [(lax.ppermute(going[0], RING, ring.shift(1)), 0)]
        left = [(lax.ppermute(going[1], RING, ring.shift(-1)), cut)]
        beside = []
        for one in packed.values():
            if len(one) == 1 and step < ring.half:
                one += other_core(ring, after(one, *going))
        if step == ring.half:
            late = exchange(after(late[1], middle), "gx")
            if out_cuts:
                beside = w_out_piece(*going)
            tokens.step(*going)
            beside = [beside, late, list(tokens.held.values())]
        if 0 not in sums and step <= ring.half - (1 if beside or step < ring.half else 0):
            while tokens.done < ring.half:
                tokens.step(*going)
            mine, theirs = in_grad_chunk(0, list(zip(early, middle, late)), *going, list(packed.values()))
            last = pack(1, *going, pres[0])
            swap_sums(0, mine, after(theirs, right, left, last))
            beside = [pres[0]]
        elif step < ring.half and in_cuts and len(packed) == len(order):
            beside = w_in_piece(*going)
    while tokens.done < ring.half:
        tokens.step()
    for number, offsets in enumerate(order):
        if number not in packed:
            pack(number)
        if len(packed[number]) == 1:
            packed[number] += other_core(ring, packed[number])
    while out_cuts:
        w_out_piece()
    while in_cuts:
        w_in_piece()
    (in_grad,) = add([0], [right + left], [(0, 0, width)])
    return (in_grad, w_in_grad[0], w_out_grad[0])


def solution(mesh):
    placed = (
        P(("gy", "gz"), "gx"),
        P("gx", ("gy", "gz")),
        P(("gy", "gz"), "gx"),
        P("gx", ("gy", "gz")),
        P(("gy", "gz"), "gx"),
    )
    return jax.shard_map(
        shards,
        mesh=mesh,
        in_specs=placed,
        out_specs=(P(("gy", "gz"), "gx"), P("gx", ("gy", "gz")), P(("gy", "gz"), "gx")),
        check_vma=False,
    )
```

```python
import math

import jax
import jax.numpy as jnp
from jax import lax
from jax.experimental import pallas as pl
from jax.experimental.pallas import tpu as pltpu
from jax.sharding import PartitionSpec as P

RING = ("gy", "gz")


class Ring:
    def __init__(self, gy, gz):
        self.cores = 2 if gy % 2 == 0 else 1
        chips = []
        for x in range(gy // self.cores):
            line = range(gz) if x % 2 == 0 else reversed(range(gz))
            chips += [(x, z) for z in line]
        self.size, self.line = len(chips), gz
        self.half = self.size // 2
        self.even = self.size % 2 == 0
        self.rank = [
            [(x * self.cores + core) * gz + z for core in range(self.cores)] for x, z in chips
        ]

    def place(self, x, z):
        return x * self.line + jnp.where(x % 2 == 0, z, self.line - 1 - z)

    def rank_at(self, place, core):
        x, z = place // self.line, place % self.line
        return (x * 2 + core) * self.line + jnp.where(x % 2 == 0, z, self.line - 1 - z)

    def shift(self, by):
        pairs = []
        for place in range(self.size):
            target = (place + by) % self.size
            for core in range(self.cores):
                pairs.append((self.rank[place][core], self.rank[target][core]))
        return pairs

    def swap(self):
        return [(ranks[core], ranks[1 - core]) for ranks in self.rank for core in range(2)]

    def groups(self):
        cut = max(self.half - 1, 1)
        return [list(range(cut)), list(range(cut, self.half + 1))]

    def offsets(self, step):
        if step == 0:
            return [0]
        if step == self.half and self.even:
            return [self.half]
        return [-step, step]


def gelu_parts(values):
    normal_cdf = 0.5 * (1.0 + lax.erf(values / math.sqrt(2.0)))
    activity = values * normal_cdf
    slope = normal_cdf + values * jnp.exp(-0.5 * values * values) / math.sqrt(2.0 * math.pi)
    return (activity, slope)


def right_trans(left, right):
    return lax.dot_general(
        left, right, (((1,), (1,)), ((), ())), preferred_element_type=jnp.float32
    )


def left_trans(left, right):
    return lax.dot_general(
        left, right, (((0,), (0,)), ((), ())), preferred_element_type=jnp.float32
    )


VMEM = pl.BlockSpec(memory_space=pltpu.VMEM)
SMEM = pl.BlockSpec(memory_space=pltpu.SMEM)
MIB = 1 << 20


def shape(rows, columns, dtype=jnp.bfloat16):
    return jax.ShapeDtypeStruct((rows, columns), dtype)


def in_hbm(rows, columns, dtype=jnp.bfloat16):
    return pltpu.HBM((rows, columns), dtype)


def constrained(arrays):
    return [pltpu.with_memory_space_constraint(each, pltpu.HBM) for each in arrays]


def cost(flops, moved, exps=0):
    return pl.CostEstimate(flops=flops, bytes_accessed=moved, transcendentals=exps)


def tile_of(total, most):
    for tile in range(most, 127, -128):
        if total % tile == 0:
            return tile
    return total


def gelu_call(ring, pres, offsets, rows):
    held, hidden = pres[0].shape
    many, count = sum(each.shape[0] for each in pres) // held, 2 * len(offsets)

    def kernel(*refs):
        given, (act_ref, slope_ref, wide) = refs[:-3], refs[-3:]
        at = 0
        for ref in given:
            wide[at : at + ref.shape[0], :] = ref[...].astype(jnp.float32)
            at += ref.shape[0]
        me, gy = lax.axis_index("gx"), lax.axis_index("gy")
        place = ring.place(gy // 2, lax.axis_index("gz"))
        for block in range(count):
            which, offset = divmod(block, len(offsets))
            there = (place + offsets[offset] + ring.size) % ring.size
            rank = ring.rank_at(there, (gy + which) % 2)
            slot = (me - rank * rows // held + many) % many
            at = pl.multiple_of(slot * held + rank * rows % held, 8)
            activity, slope = gelu_parts(wide[pl.ds(at, rows), :])
            act_ref[block * rows : (block + 1) * rows, :] = activity.astype(act_ref.dtype)
            slope_ref[block * rows : (block + 1) * rows, :] = slope

    return pl.pallas_call(
        kernel,
        grid=(1,),
        in_specs=[VMEM] * len(pres),
        out_specs=[whole(count * rows, hidden)] * 2,
        out_shape=[in_hbm(count * rows, hidden), in_hbm(count * rows, hidden, jnp.float32)],
        scratch_shapes=[pltpu.VMEM((many * held, hidden), jnp.float32)],
        cost_estimate=cost(6000 * count * rows * hidden, 1),
        compiler_params=pltpu.CompilerParams(vmem_limit_bytes=10 * MIB),
        name="gelu",
    )(*pres)


def hold_call(weights):
    rows = weights.shape[0]
    cut = rows // 4
    weights = pltpu.with_memory_space_constraint(weights, pltpu.HBM)

    def kernel(weight_ref, out_ref, here_ref, sems):
        here_ref[...] = jnp.zeros_like(here_ref)
        copies = [
            pltpu.make_async_copy(
                weight_ref.at[pl.ds(i * cut, cut)], out_ref.at[pl.ds(i * cut, cut)], sems.at[i]
            )
            for i in range(4)
        ]
        for copy in copies:
            copy.start()
        for copy in copies:
            copy.wait()

    return pl.pallas_call(
        kernel,
        in_specs=[pl.BlockSpec(memory_space=pl.ANY)],
        out_specs=[VMEM] * 2,
        out_shape=[pltpu.VMEM(weights.shape, weights.dtype), shape(8, 128, jnp.float32)],
        scratch_shapes=[pltpu.SemaphoreType.DMA((4,))],
        cost_estimate=cost(1, 1),
        compiler_params=pltpu.CompilerParams(vmem_limit_bytes=10 * MIB),
        name="hold",
    )(weights)


def whole(rows, columns):
    return pl.BlockSpec((rows, columns), lambda i: (0, 0), pipeline_mode=pl.Buffered(1))


def split_call(left, right, cut):
    def kernel(left_ref, right_ref, low_ref, high_ref):
        low_ref[...] = left_ref[:, :cut]
        high_ref[...] = right_ref[:, cut:]

    rows, width = left.shape
    return pl.pallas_call(
        kernel,
        in_specs=[VMEM] * 2,
        out_specs=[VMEM] * 2,
        out_shape=[shape(rows, cut), shape(rows, width - cut)],
        cost_estimate=cost(1, 1),
        compiler_params=pltpu.CompilerParams(vmem_limit_bytes=10 * MIB),
        name="split",
    )(left, right)


def parts_call(values):
    rows, width = values.shape
    cut = rows // 2 // 16 * 16

    def kernel(ref, upper_ref, lower_ref):
        upper_ref[...] = ref[:cut, :]
        lower_ref[...] = ref[cut:, :]

    return pl.pallas_call(
        kernel,
        in_specs=[VMEM],
        out_specs=[VMEM] * 2,
        out_shape=[shape(cut, width), shape(rows - cut, width)],
        cost_estimate=cost(1, 1),
        compiler_params=pltpu.CompilerParams(vmem_limit_bytes=10 * MIB),
        name="parts",
    )(values)


def pack_call(blocks, rows, width, space):
    flat = [piece for block in blocks for piece in block]

    def kernel(*refs):
        given, out_ref = iter(refs), refs[-1]
        for i, block in enumerate(blocks):
            at = 0
            for piece in block:
                size = piece.shape[1]
                out_ref[i * rows : (i + 1) * rows, at : at + size] = next(given)[...]
                at += size

    return pl.pallas_call(
        kernel,
        grid=(1,),
        in_specs=[VMEM] * len(flat),
        out_specs=whole(len(blocks) * rows, width) if space is pltpu.HBM else VMEM,
        out_shape=space((len(blocks) * rows, width), jnp.bfloat16),
        cost_estimate=cost(1, 1),
        compiler_params=pltpu.CompilerParams(vmem_limit_bytes=8 * MIB),
        name="pack",
    )(*flat)


def add_call(parts, arrived, rows, outs):
    width = parts[0][0].shape[1]
    flat = [each for part in parts for each in part[:2]]
    flat += [value for block in arrived for value, _ in block]

    def kernel(*refs):
        given = iter(refs[2 * len(parts) :])
        made = refs[len(refs) - len(parts) :]
        for i, ((_, _, one, other), block) in enumerate(zip(parts, arrived)):
            mine, theirs = refs[2 * i], refs[2 * i + 1]
            low = theirs[other * rows : (other + 1) * rows, :]
            made[i][...] = mine[one * rows : (one + 1) * rows, :] + low.astype(jnp.float32)
            for value, first in block:
                columns = slice(first, first + value.shape[1])
                made[i][:, columns] += next(given)[...].astype(jnp.float32)
        for ref, (i, first, last) in zip(refs[len(flat) :], outs):
            ref[...] = made[i][:, first:last].astype(ref.dtype)

    return pl.pallas_call(
        kernel,
        in_specs=[VMEM] * len(flat),
        out_specs=[VMEM] * len(outs),
        out_shape=[shape(rows, last - first) for _, first, last in outs],
        scratch_shapes=[pltpu.VMEM((rows, width), jnp.float32)] * len(parts),
        cost_estimate=cost(1, 1),
        compiler_params=pltpu.CompilerParams(vmem_limit_bytes=8 * MIB),
        name="add",
    )(*flat)


def grad_act_call(blocks, weights, rows, cuts):
    hidden, width = weights.shape
    flat = [piece for block in blocks for piece in block]
    count = len(blocks) * rows
    tile = tile_of(hidden, 256)
    steps = hidden // tile
    spans = list(zip([0] + cuts, cuts + [count]))

    def kernel(*refs):
        weight_ref, chunk_ref, part_ref, *low_refs, joined, sem = refs[len(flat) :]
        i = pl.program_id(0)
        copy = pltpu.make_async_copy(joined, chunk_ref, sem)

        @pl.when(i == 0)
        def _():
            given = iter(refs)
            for j, block in enumerate(blocks):
                at = 0
                for piece in block:
                    size = piece.shape[1]
                    joined[j * rows : (j + 1) * rows, at : at + size] = next(given)[...]
                    at += size
            copy.start()

        at = pl.ds(pl.multiple_of(i * tile, tile), tile)
        got = right_trans(joined[...], weight_ref[at, :])
        part_ref[...] = got
        for ref, (begin, end) in zip(low_refs, spans):
            ref[...] = got[begin:end].astype(ref.dtype)

        @pl.when(i == steps - 1)
        def _():
            copy.wait()

    return pl.pallas_call(
        kernel,
        grid=(steps,),
        in_specs=[VMEM] * (len(flat) + 1),
        out_specs=[
            pl.BlockSpec(memory_space=pl.ANY),
            pl.BlockSpec((count, tile), lambda i: (0, i)),
        ]
        + [pl.BlockSpec((end - begin, tile), lambda i: (0, i)) for begin, end in spans],
        out_shape=[in_hbm(count, width), in_hbm(count, hidden, jnp.float32)]
        + [(in_hbm if begin > 0 else shape)(end - begin, hidden) for begin, end in spans],
        scratch_shapes=[pltpu.VMEM((count, width), jnp.bfloat16), pltpu.SemaphoreType.DMA],
        cost_estimate=cost(1, 1),
        compiler_params=pltpu.CompilerParams(vmem_limit_bytes=10 * MIB),
        name="grad_act",
    )(*flat, weights)


def in_grad_call(part, others, slope, weights, cuts):
    flat = [piece for pieces in zip(*others) for piece in pieces]
    width, hidden = weights.shape
    count = part.shape[0]
    half = count // 2
    tile = tile_of(width, 1024)
    spans = list(zip([0] + cuts, cuts + [half]))

    def kernel(*refs):
        part_ref, slope_ref = refs[:2]
        weight_ref, pre_ref, mine_ref, *theirs_refs = refs[2 + len(flat) :]
        i = pl.program_id(0)

        @pl.when(i == 0)
        def _():
            given, at = iter(refs[2:]), 0
            for pieces in zip(*others):
                here = slice(at, at + pieces[0].shape[0])
                total = part_ref[here, :]
                for _ in pieces:
                    total = total + next(given)[...].astype(jnp.float32)
                pre_ref[here, :] = (total * slope_ref[here, :]).astype(pre_ref.dtype)
                at = here.stop

        at = pl.ds(pl.multiple_of(i * tile, tile), tile)
        got = right_trans(pre_ref[...], weight_ref[at, :])
        mine_ref[:, at] = got[:half]
        for ref, (begin, end) in zip(theirs_refs, spans):
            ref[...] = got[half + begin : half + end].astype(ref.dtype)

    return pl.pallas_call(
        kernel,
        grid=(width // tile,),
        in_specs=[whole(count, hidden)] * 2 + [whole(*each.shape) for each in flat] + [VMEM],
        out_specs=[
            whole(count, hidden),
            VMEM,
        ]
        + [pl.BlockSpec((end - begin, tile), lambda i: (0, i)) for begin, end in spans],
        out_shape=[
            in_hbm(count, hidden),
            pltpu.VMEM((half, width), jnp.float32),
        ]
        + [shape(end - begin, width) for begin, end in spans],
        cost_estimate=cost(1, 1),
        compiler_params=pltpu.CompilerParams(vmem_limit_bytes=14 * MIB),
        name="in_grad",
    )(part, slope, *flat, weights)


def pieces_of(width, most, widest=1024):
    tile = tile_of(width, widest)
    tiles = width // tile
    calls = min(most, tiles)
    ends = [tiles * i // calls for i in range(calls + 1)]
    return tile, [(first, last - first) for first, last in zip(ends, ends[1:])]


def w_out_grad_call(acts, chunks, factor, tile, first, count, earlier):
    sizes = [chunk.shape[0] for chunk in chunks]
    many, total = len(sizes), sum(sizes)
    hidden, width = earlier[0].shape if earlier else (acts[0].shape[1], chunks[0].shape[1])

    def kernel(*refs):
        given, tokens = refs[: len(acts)], refs[len(acts) : len(acts) + many]
        if earlier:
            turned, out_ref = given[0], refs[-1]
        else:
            out_ref, turned = refs[-2:]

            @pl.when(pl.program_id(0) == 0)
            def _():
                turned[...] = jnp.concatenate([ref[...] for ref in given], axis=0).T

        joined = jnp.concatenate([ref[...] for ref in tokens], axis=0)
        got = jnp.dot(turned[...], joined, preferred_element_type=jnp.float32)
        out_ref[...] = (got * factor).astype(out_ref.dtype)

    out_spec = pl.BlockSpec((hidden, tile), lambda i: (0, first + i))
    return pl.pallas_call(
        kernel,
        grid=(count,),
        in_specs=([VMEM] if earlier else [whole(*act.shape) for act in acts])
        + [pl.BlockSpec((size, tile), lambda i: (0, first + i)) for size in sizes]
        + [pl.BlockSpec(memory_space=pl.ANY)] * len(earlier),
        out_specs=[out_spec] + ([] if earlier else [whole(hidden, total)]),
        out_shape=[shape(hidden, width)] + ([] if earlier else [shape(hidden, total)]),
        input_output_aliases={len(acts) + many: 0} if earlier else {},
        cost_estimate=cost(4 * total * max(tile * count, 1024) * hidden, 2 * hidden * tile * count),
        compiler_params=pltpu.CompilerParams(vmem_limit_bytes=26 * MIB),
        name="w_out_grad",
    )(*acts, *chunks, *earlier)


def w_in_grad_call(blocks, pres, factor, tile, first, count, earlier):
    width = blocks[0].shape[1]
    many, sizes = len(blocks), [pre.shape[0] for pre in pres]
    total, hidden = sum(sizes), pres[0].shape[1]

    def kernel(*refs):
        given, wanted = refs[:many], refs[many : many + len(sizes)]
        out_ref, tokens, grads = refs[-3:]

        @pl.when(pl.program_id(0) == 0)
        def _():
            at = 0
            for ref, size in zip(wanted, sizes):
                grads[at : at + size, :] = ref[...]
                at += size

        at = 0
        for ref in given:
            tokens[at : at + ref.shape[0], :] = ref[...]
            at += ref.shape[0]
        got = left_trans(tokens[...], grads[...])
        out_ref[...] = (got * factor).astype(out_ref.dtype)

    return pl.pallas_call(
        kernel,
        grid=(count,),
        in_specs=[pl.BlockSpec((each.shape[0], tile), lambda i: (0, first + i)) for each in blocks]
        + [whole(size, hidden) for size in sizes]
        + [pl.BlockSpec(memory_space=pl.ANY)] * len(earlier),
        out_specs=pl.BlockSpec((tile, hidden), lambda i: (first + i, 0)),
        out_shape=shape(width, hidden),
        input_output_aliases={many + len(sizes): 0} if earlier else {},
        scratch_shapes=[
            pltpu.VMEM((total, tile), jnp.bfloat16),
            pltpu.VMEM((total, hidden), jnp.bfloat16),
        ],
        cost_estimate=cost(3 * total * tile * count * hidden, 2 * hidden * tile * count),
        compiler_params=pltpu.CompilerParams(vmem_limit_bytes=26 * MIB),
        name="w_in_grad",
    )(*blocks, *pres, *earlier)


def after(values, *others):
    return lax.optimization_barrier((values, others))[0]


class Gather:
    def __init__(self, ring, block, halve):
        self.ring, self.halve = ring, halve
        self.held = {0: [block]}
        self.left = self.right = block
        self.done = 0

    def step(self, *others):
        ring = self.ring
        self.done += 1
        left, right = self.left, self.right
        if others:
            left, right = after((left, right), *others)
        if self.done == ring.half and ring.even:
            if self.halve:
                cut = left.shape[1] // 2
                low, high = split_call(left, right, cut)
                low = lax.ppermute(low, RING, ring.shift(1))
                high = lax.ppermute(high, RING, ring.shift(-1))
                self.held[self.done] = [low, high]
            else:
                self.held[self.done] = [lax.ppermute(left, RING, ring.shift(1))]
        else:
            self.left = lax.ppermute(left, RING, ring.shift(1))
            self.right = lax.ppermute(right, RING, ring.shift(-1))
            self.held[-self.done], self.held[self.done] = [self.left], [self.right]


def other_core(ring, pieces):
    return [lax.ppermute(piece, RING, ring.swap()) for piece in pieces]


def exchange(values, axis):
    size = lax.axis_size(axis)
    return [
        lax.ppermute(values, axis, [(i, (i + by) % size) for i in range(size)])
        for by in range(1, size)
    ]


def shards(inputs, pre_act, out_grad, w_in, w_out):
    ring = Ring(lax.axis_size("gy"), lax.axis_size("gz"))
    assert ring.cores == 2
    rows, width = inputs.shape
    groups = ring.size * 2
    factor = 1.0 / math.sqrt(rows * groups)
    order = [[o for step in group for o in ring.offsets(step)] for group in ring.groups()]

    w_out, here = hold_call(w_out)
    upper, lower = parts_call(pre_act)
    came = [exchange(upper, "gx")]

    grads = Gather(ring, out_grad, True)
    chunks, partials, swapped = [], [], {0: other_core(ring, grads.held[0])}
    for number, offsets in enumerate(order):
        first, last = ring.groups()[number][0], ring.groups()[number][-1]
        while grads.done < last:
            if number > 0 and grads.done >= first:
                grads.step(sent, came)
            elif grads.done == 1:
                grads.step(here, swapped[0])
                came.append(exchange(after(lower, came[0], grads.held[1]), "gx"))
            else:
                earlier = [each for offset, each in swapped.items() if abs(offset) < grads.done]
                grads.step(*([earlier, came[0]] if grads.done > 1 else []))
            if number > 0 and grads.done == last:
                pres_x = [pre_act] + [each for pieces in zip(*came) for each in pieces]
                ready = after(pres_x, sent)
                acts, slopes = zip(*[gelu_call(ring, ready, each, rows) for each in order])
            for offset in ring.offsets(grads.done):
                ahead = here if number == 0 else slopes if grads.done == last else sent
                swapped[offset] = other_core(ring, after(grads.held[offset], ahead))
        blocks = [grads.held[o] for o in offsets] + [swapped[o] for o in offsets]
        cuts = [len(blocks) * rows * part // 25 // 16 * 16 for part in (10, 17)] if number == 0 else []
        if number > 0:
            blocks[0] = after(blocks[0], early)
        chunk, partial, *sent = grad_act_call(blocks, w_out, rows, cuts)
        chunks.append(chunk)
        partials.append(partial)
        if number == 0:
            early, late = exchange(sent[0], "gx"), sent[1:]
    received = [[each] for each in exchange(sent[0], "gx")]

    tokens = Gather(ring, after(inputs, grads.held[ring.half], [each for offset, each in swapped.items() if offset != ring.half]), True)
    chunks = constrained(chunks)

    def advance(*others):
        arrived = list(tokens.held.values())[1:]
        if tokens.done < ring.half:
            tokens.step(*others)
        return arrived

    tile, in_cuts = pieces_of(width, 2)
    small, out_cuts = pieces_of(width, 12, 512)
    out_cuts = [(small,) + cut for cut in out_cuts]
    if len(out_cuts) == 12:
        out_cuts = [(small, 11, 1), (2 * small, 0, 3), (small, 6, 5)]
    w_out_grad, w_in_grad, turned = [], [], None

    def w_out_piece(*others):
        nonlocal w_out_grad, turned
        out_tile, first, count = out_cuts.pop(0)
        given = list(acts) if turned is None else [turned]
        given[0] = after(given[0], *others)
        got = w_out_grad_call(given, chunks, factor, out_tile, first, count, w_out_grad)
        w_out_grad = got[:1]
        if turned is None:
            turned = got[1]
        return w_out_grad

    def w_in_piece(*others):
        nonlocal w_in_grad
        first, count = in_cuts.pop(0)
        flat = [each for number in range(len(order)) for each in packed[number]]
        given = [after(pres[0], *others)] + pres[1:]
        w_in_grad = [w_in_grad_call(flat, given, factor, tile, first, count, w_in_grad)]
        return w_in_grad

    w_out_piece(advance(), early)
    arrived = advance()
    w_in = pltpu.with_memory_space_constraint(w_in, pltpu.VMEM)
    if len(out_cuts) > 1:
        w_out_piece(arrived)

    sums, pres = {}, [None] * len(order)

    def in_grad_chunk(i, received, *others):
        partial = after(partials[i], *others)
        cuts = [(len(order[i]) - 2) * rows] if i == 0 and len(order[i]) > 2 else []
        pres[i], mine, *theirs = in_grad_call(partial, received, slopes[i], w_in, cuts)
        return mine, theirs

    def swap_sums(i, mine, theirs):
        place = len(order[i])
        for piece in reversed(theirs):
            got = lax.ppermute(piece, RING, ring.swap())
            for other in reversed(range(piece.shape[0] // rows)):
                place -= 1
                sums[order[i][place]] = (mine, got, place, other)

    def add(offsets, arrived, outs, *others):
        parts = [sums[offset] for offset in offsets]
        parts[0] = (parts[0][0], after(parts[0][1], *others)) + parts[0][2:]
        return add_call(parts, arrived, rows, outs)

    packed = {}

    def pack(number, *others):
        blocks = after([tokens.held[o] for o in order[number]], *others)
        space = pltpu.HBM if number == 0 else pltpu.VMEM
        packed[number] = [pack_call(blocks, rows, width, space)]
        return packed[number]

    mine, theirs = in_grad_chunk(1, received, w_out_grad, advance(*w_out_grad))
    middle = exchange(after(late[0], received), "gx")
    if order[0][-1] in tokens.held:
        pack(0, pres[1])
    swap_sums(1, mine, after(theirs, list(tokens.held.values()), middle, list(packed.values())))
    right, left, beside = [], [], []
    for step in range(ring.half, 0, -1):
        if step == ring.half and ring.even:
            cut = width // 2
            outs = [(0, 0, cut), (0, cut, width)]
            going = add([step], [[]], outs, beside)
        else:
            cut = 0
            outs = [(0, 0, width), (1, 0, width)]
            going = add([step, -step], [right, left], outs, beside)
        right = [(lax.ppermute(going[0], RING, ring.shift(1)), 0)]
        left = [(lax.ppermute(going[1], RING, ring.shift(-1)), cut)]
        beside = []
        for one in packed.values():
            if len(one) == 1 and step < ring.half:
                one += other_core(ring, after(one, *going))
        if step == ring.half:
            late = exchange(after(late[1], middle), "gx")
            if out_cuts:
                beside = w_out_piece(*going)
            tokens.step(*going)
            beside = [beside, late, list(tokens.held.values())]
        if 0 not in sums and step <= ring.half - (1 if beside or step < ring.half else 0):
            while tokens.done < ring.half:
                tokens.step(*going)
            mine, theirs = in_grad_chunk(0, list(zip(early, middle, late)), *going, list(packed.values()))
            last = pack(1, *going, pres[0])
            swap_sums(0, mine, after(theirs, right, left, last))
            beside = [pres[0]]
        elif step < ring.half and in_cuts and len(packed) == len(order):
            beside = w_in_piece(*going)
    while tokens.done < ring.half:
        tokens.step()
    for number, offsets in enumerate(order):
        if number not in packed:
            pack(number)
        if len(packed[number]) == 1:
            packed[number] += other_core(ring, packed[number])
    while out_cuts:
        w_out_piece()
    while in_cuts:
        w_in_piece()
    (in_grad,) = add([0], [right + left], [(0, 0, width)])
    return (in_grad, w_in_grad[0], w_out_grad[0])


def solution(mesh):
    placed = (
        P(("gy", "gz"), "gx"),
        P("gx", ("gy", "gz")),
        P(("gy", "gz"), "gx"),
        P("gx", ("gy", "gz")),
        P(("gy", "gz"), "gx"),
    )
    return jax.shard_map(
        shards,
        mesh=mesh,
        in_specs=placed,
        out_specs=(P(("gy", "gz"), "gx"), P("gx", ("gy", "gz")), P(("gy", "gz"), "gx")),
        check_vma=False,
    )
```
